32 devices in a mesh: seq: 8 (over z, y), tp: 4 (over x, core).
Axes of the slice: x: 2, y: 2, z: 4, core: 2. Of those that a mesh axis runs over, the one named last changes fastest.
Arguments:
- subsampled: bfloat16 [2048, 4096], P('seq'), may hold values from -6 to 6
- proj_weight: bfloat16 [4096, 1024], P(None, 'tp'), may hold values from -0.09375 to 0.09375
- value_weight: bfloat16 [1024, 1024], P(None, 'tp'), may hold values from -0.1875 to 0.1875
- gate_weight: bfloat16 [1024, 1024], P(None, 'tp'), may hold values from -0.1875 to 0.1875
- conv_kernel: float32 [9, 1024], P(None, 'tp'), may hold values from -2 to 2
- bn_gain: float32 [1024], P('tp'), may hold values from 0.5 to 1.5
- bn_shift: float32 [1024], P('tp'), may hold values from -2 to 2
- down_weight: bfloat16 [1024, 1024], P(None, 'tp'), may hold values from -0.1875 to 0.1875
- clip_frames: int32 [8, 8], replicated, may hold values from 1 to 64, 256 in all within a row
- clip_dest: int32 [8, 8], replicated, may hold values from 0 to 7, each once within a row
- out_grad: bfloat16 [4096, 1024], P('seq', 'tp'), may hold values from -0.13183594 to 0.13183594
Outputs:
- block_out: bfloat16 [4096, 1024], P('seq', 'tp')
- proj_grad: float32 [4096, 1024], P('seq', 'tp')
- value_grad: float32 [1024, 1024], P('seq', 'tp')
- gate_grad: float32 [1024, 1024], P('seq', 'tp')
- down_grad: float32 [1024, 1024], P('seq', 'tp')
- bn_gain_grad: float32 [1024], P('tp')
- bn_shift_grad: float32 [1024], P('tp')
The draws below stay inside these ranges and needn't reach their ends.
Inputs may be any that keep to these rules, and one draw needn't show every extreme that they name: `clip_frames`: row s holds the frame counts of the 8 clips of owner s, summing to 256; the largest of each row is 64. `clip_dest`: each row is a permutation: owner s sends exactly one clip to every packed shard.
All inputs are finite; a program needn't handle non-finite values.
Results may differ from the reference program's by a relative error of at most 0.0077.
Values may be sent and summed in bfloat16 or wider, within the bound.
A program may use at most 192 MiB of HBM per device.

```python
import math
import jax
import jax.numpy as jnp
import numpy as np
from jax import lax

D = 1024
SUB_WIDTH = 4096
KERNEL = 9
MOST = 64
OWN_ROWS = 256
ALL_ROWS = 2048
PACKED = 4096
N_SEQ = 8


def shard_levels(own_key, extent, pieces, low, top_value):
    def one(position, shards_of):
        steps = jax.random.uniform(jax.random.fold_in(jax.random.fold_in(own_key, 6), position), (shards_of,), jnp.float32, low / len(pieces), top_value / len(pieces))
        return jnp.repeat(jnp.exp(steps), extent[position] // shards_of).reshape((-1,) + (1,) * (len(extent) - position - 1))

    level = one(*pieces[0])
    for cut in pieces[1:]:
        level = level * one(*cut)
    return level


def profile(number_of, total, most, skew):
    weights = [(1 << 20) // math.isqrt(rank ** skew) + 1 for rank in range(2, number_of + 1)]
    spare, given = total - most - (number_of - 1), [1] * (number_of - 1)
    while spare > 0:
        movable = [i for i in range(number_of - 1) if given[i] < most]
        pool, budget = sum([weights[i] for i in movable]), spare
        for i in movable:
            extra = min(most - given[i], max(1, budget * weights[i] // pool), spare)
            given[i] = given[i] + extra
            spare = spare - extra
    return np.array([most] + given)


def uneven_parts(key, number_of, total, most, slope):
    if number_of == 2:
        one = jax.random.randint(key, (), max(1, total - most), min(most, total - 1) + 1)
        return jnp.stack([one, total - one])
    tallies = jnp.asarray(profile(number_of, total, most, slope), jnp.int32)
    pairs = (number_of - 1) // 2
    donor, sink = tallies[1:1 + 2 * pairs:2], tallies[2:2 + 2 * pairs:2]
    margin = jnp.minimum(donor - 1, most - sink)
    passed = jax.random.randint(jax.random.fold_in(key, 1), (pairs,), 0, 1 << 20) % (margin + 1)
    tallies = tallies.at[1:1 + 2 * pairs:2].set(donor - passed).at[2:2 + 2 * pairs:2].set(sink + passed)
    return tallies[jax.random.permutation(jax.random.fold_in(key, 2), number_of)]


def bell_draw(own_key, extent, scale, bound, cuts=(), held_as=jnp.bfloat16):
    factor_of = shard_levels(own_key, extent, cuts, -0.22, 0.18) if cuts else 1.0
    drawn = jax.random.normal(own_key, extent, jnp.float32) * scale * factor_of
    return jnp.minimum(jnp.maximum(drawn, -bound), bound).astype(held_as)


def setup_inputs(seed: int = 0) -> dict:
    keys = jax.random.split(jax.random.key(seed), 12)
    subsampled = bell_draw(keys[0], (ALL_ROWS, SUB_WIDTH), 1.0, 6.0, ((0, 8),))
    proj_weight = bell_draw(keys[1], (SUB_WIDTH, D), SUB_WIDTH ** -0.5, 0.09375, ((1, 4),))
    value_weight = bell_draw(keys[2], (D, D), D ** -0.5, 0.1875, ((1, 4),))
    gate_weight = bell_draw(keys[3], (D, D), D ** -0.5, 0.1875, ((1, 4),))
    conv_kernel = bell_draw(keys[4], (KERNEL, D), 0.33, 2.0, ((1, 4),), jnp.float32)
    bn_gain = jnp.clip(0.5 + 1.0 * jax.random.uniform(keys[5], (D,), jnp.float32) ** shard_levels(keys[5], (D,), ((0, 4),), -0.2, 0.2), 0.5, 1.5)
    bn_shift = bell_draw(keys[6], (D,), 0.5, 2.0, ((0, 4),), jnp.float32)
    down_weight = bell_draw(keys[7], (D, D), D ** -0.5, 0.1875, ((1, 4),))
    clip_frames = jax.vmap(lambda own: uneven_parts(own, N_SEQ, OWN_ROWS, MOST, 1))(jax.random.split(keys[8], N_SEQ)).reshape((N_SEQ, N_SEQ)).astype(jnp.int32)
    clip_dest = jax.vmap(lambda own: jax.random.permutation(own, N_SEQ))(jax.random.split(keys[9], N_SEQ)).reshape((N_SEQ, N_SEQ)).astype(jnp.int32)
    out_grad = bell_draw(keys[10], (PACKED, D), ((N_SEQ * OWN_ROWS) ** -0.5), 0.13183594, ((0, 8), (1, 4)))
    return dict(subsampled=subsampled, proj_weight=proj_weight, value_weight=value_weight, gate_weight=gate_weight, conv_kernel=conv_kernel, bn_gain=bn_gain, bn_shift=bn_shift, down_weight=down_weight, clip_frames=clip_frames, clip_dest=clip_dest, out_grad=out_grad)


def depthwise(field, kernel):
    half = kernel.shape[0] // 2
    length = field.shape[1]
    padded = jnp.pad(field, ((0, 0), (half, half), (0, 0)))
    total = jnp.zeros(field.shape, jnp.float32)
    for offset in range(kernel.shape[0]):
        total = total + kernel[offset] * padded[:, offset:offset + length]
    return total

def depthwise_back(grad, kernel):
    half = kernel.shape[0] // 2
    length = grad.shape[1]
    padded = jnp.pad(grad, ((0, 0), (half, half), (0, 0)))
    total = jnp.zeros(grad.shape, jnp.float32)
    for offset in range(kernel.shape[0]):
        begin = 2 * half - offset
        total = total + kernel[offset] * padded[:, begin:begin + length]
    return total

def reference(subsampled, proj_weight, value_weight, gate_weight, conv_kernel, bn_gain, bn_shift, down_weight, clip_frames, clip_dest, out_grad):
    shards = clip_frames.shape[0]
    width = proj_weight.shape[1]
    offsets = jnp.cumsum(clip_frames, axis=1) - clip_frames
    match = clip_dest[None, :, :] == jnp.arange(shards, dtype=jnp.int32)[:, None, None]
    starts = lax.optimization_barrier(jnp.sum(jnp.where(match, offsets[None], 0), axis=2)).astype(jnp.int32)
    lengths = lax.optimization_barrier(jnp.sum(jnp.where(match, clip_frames[None], 0), axis=2)).astype(jnp.int32)
    frame_pos = jnp.arange(MOST, dtype=jnp.int32)
    owners = jnp.arange(shards, dtype=jnp.int32)
    rows = owners[None, :, None] * OWN_ROWS + starts[:, :, None] + frame_pos[None, None, :]
    rows = jnp.minimum(rows, shards * OWN_ROWS - 1).reshape(-1).astype(jnp.int32)
    valid = (frame_pos[None, None, :] < lengths[:, :, None]).reshape(-1, 1)
    mask = valid.astype(jnp.float32)
    count = float(ALL_ROWS)
    projected = jnp.dot(subsampled, proj_weight, preferred_element_type=jnp.float32).astype(jnp.bfloat16)
    hidden = jnp.where(valid, jnp.take(projected, rows, axis=0), jnp.zeros((), jnp.bfloat16))
    hidden32 = hidden.astype(jnp.float32)
    centred = hidden32 - lax.optimization_barrier(jnp.mean(hidden32, axis=1, keepdims=True))
    sigma = jnp.sqrt(lax.optimization_barrier(jnp.mean(centred * centred, axis=1, keepdims=True)) + 1e-05)
    normed = centred / sigma
    normed16 = normed.astype(jnp.bfloat16)
    value_pre = jnp.dot(normed16, value_weight, preferred_element_type=jnp.float32)
    gate_pre = jnp.dot(normed16, gate_weight, preferred_element_type=jnp.float32)
    gate_sig = jax.nn.sigmoid(gate_pre)
    glu = value_pre * gate_sig * mask
    slots = shards * shards
    conv = depthwise(glu.reshape(slots, MOST, width), conv_kernel).reshape(-1, width)
    conv_mean = lax.optimization_barrier(jnp.sum(conv * mask, axis=0)) / count
    conv_var = lax.optimization_barrier(jnp.sum(conv * conv * mask, axis=0)) / count - conv_mean * conv_mean
    bn_scale = jnp.sqrt(conv_var + 1e-05)
    bn_hat = (conv - conv_mean) / bn_scale
    batch_normed = bn_gain * bn_hat + bn_shift
    bn_sig = jax.nn.sigmoid(batch_normed)
    swish = (batch_normed * bn_sig).astype(jnp.bfloat16)
    mixed = jnp.dot(swish, down_weight.T, preferred_element_type=jnp.float32)
    block_out = ((hidden32 + mixed) * mask).astype(jnp.bfloat16)
    grad_out = jnp.where(valid, out_grad, jnp.zeros((), jnp.bfloat16))
    down_grad = jnp.dot(grad_out.T, swish, preferred_element_type=jnp.float32)
    grad_swish = jnp.dot(grad_out, down_weight, preferred_element_type=jnp.float32)
    grad_bn = grad_swish * bn_sig * (1.0 + batch_normed * (1.0 - bn_sig)) * mask
    bn_shift_grad = lax.optimization_barrier(jnp.sum(grad_bn, axis=0))
    bn_gain_grad = lax.optimization_barrier(jnp.sum(grad_bn * bn_hat, axis=0))
    grad_conv = bn_gain / bn_scale * (grad_bn - (bn_shift_grad + bn_hat * bn_gain_grad) / count) * mask
    grad_glu = depthwise_back(grad_conv.reshape(slots, MOST, width), conv_kernel).reshape(-1, width) * mask
    grad_value = (grad_glu * gate_sig).astype(jnp.bfloat16)
    grad_gate = (grad_glu * value_pre * gate_sig * (1.0 - gate_sig)).astype(jnp.bfloat16)
    value_grad = jnp.dot(normed16.T, grad_value, preferred_element_type=jnp.float32)
    gate_grad = jnp.dot(normed16.T, grad_gate, preferred_element_type=jnp.float32)
    grad_normed = jnp.dot(grad_value, value_weight.T, preferred_element_type=jnp.float32) + jnp.dot(grad_gate, gate_weight.T, preferred_element_type=jnp.float32)
    grad_hidden = (grad_normed - lax.optimization_barrier(jnp.mean(grad_normed, axis=1, keepdims=True)) - normed * lax.optimization_barrier(jnp.mean(grad_normed * normed, axis=1, keepdims=True))) / sigma
    grad_packed = ((grad_out.astype(jnp.float32) + grad_hidden) * mask).astype(jnp.bfloat16)
    grad_proj = jnp.zeros((shards * OWN_ROWS, width), jnp.bfloat16).at[rows].add(grad_packed)
    proj_grad = jnp.dot(subsampled.T, grad_proj, preferred_element_type=jnp.float32)
    return (block_out, proj_grad, value_grad, gate_grad, down_grad, bn_gain_grad, bn_shift_grad)
```

```python
import jax
import jax.numpy as jnp
from jax import lax
from jax.sharding import PartitionSpec as P

MOST = 64


def depthwise(field, kernel):
    half = kernel.shape[0] // 2
    length = field.shape[1]
    padded = jnp.pad(field, ((0, 0), (half, half), (0, 0)))
    total = jnp.zeros(field.shape, jnp.float32)
    for offset in range(kernel.shape[0]):
        total = total + kernel[offset] * padded[:, offset : offset + length]
    return total


def depthwise_back(grad, kernel):
    half = kernel.shape[0] // 2
    length = grad.shape[1]
    padded = jnp.pad(grad, ((0, 0), (half, half), (0, 0)))
    total = jnp.zeros(grad.shape, jnp.float32)
    for offset in range(kernel.shape[0]):
        begin = 2 * half - offset
        total = total + kernel[offset] * padded[:, begin : begin + length]
    return total


def contract_rows(left, right):
    return lax.dot_general(
        left, right, (((0,), (0,)), ((), ())), preferred_element_type=jnp.float32
    )


def contract_cols(left, right):
    return lax.dot_general(
        left, right, (((1,), (1,)), ((), ())), preferred_element_type=jnp.float32
    )


def body(
    subsampled,
    proj_weight,
    value_weight,
    gate_weight,
    conv_kernel,
    bn_gain,
    bn_shift,
    down_weight,
    clip_frames,
    clip_dest,
    out_grad,
):
    shards = lax.axis_size("seq")
    seq_index = lax.axis_index("seq")
    tp_index = lax.axis_index("tp")
    own_rows = subsampled.shape[0]
    part_width = proj_weight.shape[1]
    count = float(own_rows * shards)
    clip_lens = lax.dynamic_slice_in_dim(clip_frames, seq_index, 1, 0)[0]
    clip_targets = lax.dynamic_slice_in_dim(clip_dest, seq_index, 1, 0)[0]
    shard_ids = jnp.arange(shards, dtype=jnp.int32)
    earlier = shard_ids[None, :] < shard_ids[:, None]
    offsets = jnp.sum(jnp.where(earlier, clip_lens[None, :], 0), axis=1)
    match = clip_targets[None, :] == shard_ids[:, None]
    starts = jnp.sum(jnp.where(match, offsets[None, :], 0), axis=1)
    lengths = jnp.sum(jnp.where(match, clip_lens[None, :], 0), axis=1)
    frame_pos = jnp.arange(MOST, dtype=jnp.int32)
    source_rows = jnp.minimum(starts[:, None] + frame_pos[None, :], own_rows - 1).reshape(-1)
    send_valid = (frame_pos[None, :] < lengths[:, None]).reshape(-1, 1)
    projected = jnp.dot(subsampled, proj_weight, preferred_element_type=jnp.float32).astype(
        jnp.bfloat16
    )
    outgoing = jnp.where(
        send_valid, jnp.take(projected, source_rows, axis=0), jnp.zeros((), jnp.bfloat16)
    )
    arrived = lax.all_to_all(
        outgoing.reshape(shards, MOST, part_width), "seq", split_axis=0, concat_axis=0, tiled=True
    )
    hidden_part = arrived.reshape(shards * MOST, part_width)
    hidden_full = lax.all_gather(hidden_part, "tp", axis=1, tiled=True)
    incoming = clip_dest == seq_index
    in_lengths = jnp.sum(jnp.where(incoming, clip_frames, 0), axis=1)
    valid = (frame_pos[None, :] < in_lengths[:, None]).reshape(-1, 1)
    mask = valid.astype(jnp.float32)
    hidden32 = hidden_full.astype(jnp.float32)
    centred = hidden32 - jnp.mean(hidden32, axis=1, keepdims=True)
    sigma = jnp.sqrt(jnp.mean(centred * centred, axis=1, keepdims=True) + 1e-05)
    normed = centred / sigma
    normed16 = normed.astype(jnp.bfloat16)
    value_pre = jnp.dot(normed16, value_weight, preferred_element_type=jnp.float32)
    gate_pre = jnp.dot(normed16, gate_weight, preferred_element_type=jnp.float32)
    gate_sig = jax.nn.sigmoid(gate_pre)
    glu = value_pre * gate_sig * mask
    conv = depthwise(glu.reshape(shards, MOST, part_width), conv_kernel).reshape(-1, part_width)
    conv_total, square_total = lax.psum(
        (jnp.sum(conv * mask, axis=0), jnp.sum(conv * conv * mask, axis=0)), "seq"
    )
    conv_mean = conv_total / count
    conv_var = square_total / count - conv_mean * conv_mean
    bn_scale = jnp.sqrt(conv_var + 1e-05)
    bn_hat = (conv - conv_mean) / bn_scale
    batch_normed = bn_gain * bn_hat + bn_shift
    bn_sig = jax.nn.sigmoid(batch_normed)
    swish = (batch_normed * bn_sig).astype(jnp.bfloat16)
    mixed = lax.psum_scatter(
        contract_cols(swish, down_weight), "tp", scatter_dimension=1, tiled=True
    )
    block_out = ((hidden_part.astype(jnp.float32) + mixed) * mask).astype(jnp.bfloat16)
    grad_out = jnp.where(valid, out_grad, jnp.zeros((), jnp.bfloat16))
    grad_full = lax.all_gather(grad_out, "tp", axis=1, tiled=True)
    down_local = contract_rows(grad_full, swish)
    grad_swish = jnp.dot(grad_full, down_weight, preferred_element_type=jnp.float32)
    grad_bn = grad_swish * bn_sig * (1.0 + batch_normed * (1.0 - bn_sig)) * mask
    bn_shift_grad, bn_gain_grad = lax.psum(
        (jnp.sum(grad_bn, axis=0), jnp.sum(grad_bn * bn_hat, axis=0)), "seq"
    )
    grad_conv = (
        bn_gain / bn_scale * (grad_bn - (bn_shift_grad + bn_hat * bn_gain_grad) / count) * mask
    )
    grad_glu = (
        depthwise_back(grad_conv.reshape(shards, MOST, part_width), conv_kernel).reshape(
            -1, part_width
        )
        * mask
    )
    grad_value = (grad_glu * gate_sig).astype(jnp.bfloat16)
    grad_gate = (grad_glu * value_pre * gate_sig * (1.0 - gate_sig)).astype(jnp.bfloat16)
    value_local = contract_rows(normed16, grad_value)
    gate_local = contract_rows(normed16, grad_gate)
    normed_terms = contract_cols(grad_value, value_weight) + contract_cols(grad_gate, gate_weight)
    grad_normed = lax.psum(normed_terms, "tp")
    grad_hidden = (
        grad_normed
        - jnp.mean(grad_normed, axis=1, keepdims=True)
        - normed * jnp.mean(grad_normed * normed, axis=1, keepdims=True)
    ) / sigma
    grad_hidden = lax.dynamic_slice_in_dim(grad_hidden, tp_index * part_width, part_width, 1)
    grad_packed = ((grad_out.astype(jnp.float32) + grad_hidden) * mask).astype(jnp.bfloat16)
    returned = lax.all_to_all(
        grad_packed.reshape(shards, MOST, part_width),
        "seq",
        split_axis=0,
        concat_axis=0,
        tiled=True,
    )
    row_ids = jnp.arange(own_rows, dtype=jnp.int32)
    clip_ends = offsets + clip_lens
    clip_of_row = jnp.sum((clip_ends[None, :] <= row_ids[:, None]).astype(jnp.int32), axis=1)
    row_match = clip_of_row[:, None] == shard_ids[None, :]
    row_start = jnp.sum(jnp.where(row_match, offsets[None, :], 0), axis=1)
    row_target = jnp.sum(jnp.where(row_match, clip_targets[None, :], 0), axis=1)
    positions = row_target * MOST + row_ids - row_start
    grad_proj = jnp.take(returned.reshape(shards * MOST, part_width), positions, axis=0)
    proj_local = contract_rows(subsampled, grad_proj)
    proj_grad, value_grad, gate_grad, down_grad = (
        lax.psum_scatter(proj_local, "seq", scatter_dimension=0, tiled=True),
        lax.psum_scatter(value_local, "seq", scatter_dimension=0, tiled=True),
        lax.psum_scatter(gate_local, "seq", scatter_dimension=0, tiled=True),
        lax.psum_scatter(down_local, "seq", scatter_dimension=0, tiled=True),
    )
    return (block_out, proj_grad, value_grad, gate_grad, down_grad, bn_gain_grad, bn_shift_grad)


def solution(mesh):
    placed = (
        P("seq", None),
        P(None, "tp"),
        P(None, "tp"),
        P(None, "tp"),
        P(None, "tp"),
        P("tp"),
        P("tp"),
        P(None, "tp"),
        P(),
        P(),
        P("seq", "tp"),
    )
    return jax.shard_map(
        body,
        mesh=mesh,
        in_specs=placed,
        out_specs=(
            P("seq", "tp"),
            P("seq", "tp"),
            P("seq", "tp"),
            P("seq", "tp"),
            P("seq", "tp"),
            P("tp"),
            P("tp"),
        ),
        check_vma=False,
    )
```

```python
import functools
import jax
import jax.numpy as jnp
from jax import lax
from jax.experimental import pallas as pl
from jax.experimental.pallas import tpu as pltpu
from jax.sharding import PartitionSpec as P

MOST = 64


def source_of(kind, ref, index):
    if kind == "rows":
        return ref.at[index]
    if kind == "split":
        width = ref.shape[1] // lax.axis_size("tp")
        return ref.at[:, pl.ds(pl.multiple_of(index * width, 128), width)]
    return ref


def target_of(kind, ref, index, width):
    if kind == "columns":
        return ref.at[:, pl.ds(pl.multiple_of(index * width, 128), width)]
    return ref.at[index]


def transfer_kernel(plan, *refs):
    count = len(plan)
    sources, targets = refs[:count], refs[count : 2 * count]
    sends, recvs, local_sem = refs[2 * count : 3 * count], refs[3 * count : 4 * count], refs[4 * count]
    barrier = pltpu.get_barrier_semaphore()
    greeted = 0
    for axis in sorted({axis for _, axis in plan}):
        size = lax.axis_size(axis)
        me = lax.axis_index(axis)
        for step in range(1, size):
            peer = lax.rem(me + step, size)
            pl.semaphore_signal(
                barrier, inc=1, device_id={axis: peer}, device_id_type=pl.DeviceIdType.MESH
            )
        greeted += size - 1
    pl.semaphore_wait(barrier, greeted)
    copies = []
    for which, (kind, axis) in enumerate(plan):
        size = lax.axis_size(axis)
        me = lax.axis_index(axis)
        source, target = sources[which], targets[which]
        width = source.shape[-1]
        for step in range(1, size):
            peer = lax.rem(me + step, size)
            copy = pltpu.make_async_remote_copy(
                src_ref=source_of(kind, source, peer),
                dst_ref=target_of(kind, target, me, width),
                send_sem=sends[which].at[step],
                recv_sem=recvs[which].at[step],
                device_id={axis: peer},
                device_id_type=pl.DeviceIdType.MESH,
            )
            copy.start()
            copies.append(copy)
        own = pltpu.make_async_copy(
            source_of(kind, source, me), target_of(kind, target, me, width), local_sem.at[which]
        )
        own.start()
        copies.append(own)
    for copy in copies:
        copy.wait()


def transfer(number, *items):
    plan = tuple((kind, axis) for kind, axis, _ in items)
    arrays = [array for _, _, array in items]
    outs = []
    for kind, axis, array in items:
        size = lax.axis_size(axis)
        if kind == "rows":
            shape = array.shape
        elif kind == "split":
            shape = (size, array.shape[0], array.shape[1] // size)
        elif kind == "columns":
            shape = (array.shape[0], array.shape[1] * size)
        else:
            shape = (size,) + array.shape
        outs.append(jax.ShapeDtypeStruct(shape, array.dtype))
    sems = [pltpu.SemaphoreType.DMA((lax.axis_size(axis),)) for _, axis in plan]
    return pl.pallas_call(
        functools.partial(transfer_kernel, plan),
        out_shape=outs,
        in_specs=[pl.BlockSpec(memory_space=pl.ANY)] * len(arrays),
        out_specs=[pl.BlockSpec(memory_space=pl.ANY)] * len(arrays),
        scratch_shapes=sems + sems + [pltpu.SemaphoreType.DMA((len(plan),))],
        compiler_params=pltpu.CompilerParams(collective_id=number, has_side_effects=True),
    )(*arrays)


def summed(parts):
    return jnp.sum(parts.astype(jnp.float32), axis=0)


def stacked(first, second):
    empty = jnp.zeros((6,) + first.shape, jnp.float32)
    return jnp.concatenate([first[None], second[None], empty], axis=0)


def depthwise(field, kernel):
    half = kernel.shape[0] // 2
    length = field.shape[1]
    padded = jnp.pad(field, ((0, 0), (half, half), (0, 0)))
    total = jnp.zeros(field.shape, jnp.float32)
    for offset in range(kernel.shape[0]):
        total = total + kernel[offset] * padded[:, offset : offset + length]
    return total


def depthwise_back(grad, kernel):
    half = kernel.shape[0] // 2
    length = grad.shape[1]
    padded = jnp.pad(grad, ((0, 0), (half, half), (0, 0)))
    total = jnp.zeros(grad.shape, jnp.float32)
    for offset in range(kernel.shape[0]):
        begin = 2 * half - offset
        total = total + kernel[offset] * padded[:, begin : begin + length]
    return total


def contract_rows(left, right):
    return lax.dot_general(
        left, right, (((0,), (0,)), ((), ())), preferred_element_type=jnp.float32
    )


def contract_cols(left, right):
    return lax.dot_general(
        left, right, (((1,), (1,)), ((), ())), preferred_element_type=jnp.float32
    )


def body(
    subsampled,
    proj_weight,
    value_weight,
    gate_weight,
    conv_kernel,
    bn_gain,
    bn_shift,
    down_weight,
    clip_frames,
    clip_dest,
    out_grad,
):
    shards = lax.axis_size("seq")
    seq_index = lax.axis_index("seq")
    tp_index = lax.axis_index("tp")
    own_rows = subsampled.shape[0]
    part_width = proj_weight.shape[1]
    count = float(own_rows * shards)
    clip_lens = lax.dynamic_slice_in_dim(clip_frames, seq_index, 1, 0)[0]
    clip_targets = lax.dynamic_slice_in_dim(clip_dest, seq_index, 1, 0)[0]
    shard_ids = jnp.arange(shards, dtype=jnp.int32)
    earlier = shard_ids[None, :] < shard_ids[:, None]
    offsets = jnp.sum(jnp.where(earlier, clip_lens[None, :], 0), axis=1)
    match = clip_targets[None, :] == shard_ids[:, None]
    starts = jnp.sum(jnp.where(match, offsets[None, :], 0), axis=1)
    lengths = jnp.sum(jnp.where(match, clip_lens[None, :], 0), axis=1)
    frame_pos = jnp.arange(MOST, dtype=jnp.int32)
    source_rows = jnp.minimum(starts[:, None] + frame_pos[None, :], own_rows - 1).reshape(-1)
    send_valid = (frame_pos[None, :] < lengths[:, None]).reshape(-1, 1)
    projected = jnp.dot(subsampled, proj_weight, preferred_element_type=jnp.float32).astype(
        jnp.bfloat16
    )
    outgoing = jnp.where(
        send_valid, jnp.take(projected, source_rows, axis=0), jnp.zeros((), jnp.bfloat16)
    )
    incoming = clip_dest == seq_index
    in_lengths = jnp.sum(jnp.where(incoming, clip_frames, 0), axis=1)
    valid = (frame_pos[None, :] < in_lengths[:, None]).reshape(-1, 1)
    mask = valid.astype(jnp.float32)
    grad_out = jnp.where(valid, out_grad, jnp.zeros((), jnp.bfloat16))
    arrived, grad_full = transfer(
        1,
        ("rows", "seq", outgoing.reshape(shards, MOST, part_width)),
        ("columns", "tp", grad_out),
    )
    hidden_part = arrived.reshape(shards * MOST, part_width)
    (hidden_full,) = transfer(2, ("columns", "tp", hidden_part))
    hidden32 = hidden_full.astype(jnp.float32)
    centred = hidden32 - jnp.mean(hidden32, axis=1, keepdims=True)
    sigma = jnp.sqrt(jnp.mean(centred * centred, axis=1, keepdims=True) + 1e-05)
    normed = centred / sigma
    normed16 = normed.astype(jnp.bfloat16)
    value_pre = jnp.dot(normed16, value_weight, preferred_element_type=jnp.float32)
    gate_pre = jnp.dot(normed16, gate_weight, preferred_element_type=jnp.float32)
    gate_sig = jax.nn.sigmoid(gate_pre)
    glu = value_pre * gate_sig * mask
    conv = depthwise(glu.reshape(shards, MOST, part_width), conv_kernel).reshape(-1, part_width)
    (conv_parts,) = transfer(
        3, ("whole", "seq", stacked(jnp.sum(conv * mask, axis=0), jnp.sum(conv * conv * mask, axis=0)))
    )
    conv_sums = summed(conv_parts)
    conv_total, square_total = conv_sums[0], conv_sums[1]
    conv_mean = conv_total / count
    conv_var = square_total / count - conv_mean * conv_mean
    bn_scale = jnp.sqrt(conv_var + 1e-05)
    bn_hat = (conv - conv_mean) / bn_scale
    batch_normed = bn_gain * bn_hat + bn_shift
    bn_sig = jax.nn.sigmoid(batch_normed)
    swish = (batch_normed * bn_sig).astype(jnp.bfloat16)
    mixed_local = contract_cols(swish, down_weight).astype(jnp.bfloat16)
    down_local = contract_rows(grad_full, swish)
    grad_swish = jnp.dot(grad_full, down_weight, preferred_element_type=jnp.float32)
    grad_bn = grad_swish * bn_sig * (1.0 + batch_normed * (1.0 - bn_sig)) * mask
    (bn_parts,) = transfer(
        4, ("whole", "seq", stacked(jnp.sum(grad_bn, axis=0), jnp.sum(grad_bn * bn_hat, axis=0)))
    )
    bn_sums = summed(bn_parts)
    bn_shift_grad, bn_gain_grad = bn_sums[0], bn_sums[1]
    grad_conv = (
        bn_gain / bn_scale * (grad_bn - (bn_shift_grad + bn_hat * bn_gain_grad) / count) * mask
    )
    grad_glu = (
        depthwise_back(grad_conv.reshape(shards, MOST, part_width), conv_kernel).reshape(
            -1, part_width
        )
        * mask
    )
    grad_value = (grad_glu * gate_sig).astype(jnp.bfloat16)
    grad_gate = (grad_glu * value_pre * gate_sig * (1.0 - gate_sig)).astype(jnp.bfloat16)
    value_local = contract_rows(normed16, grad_value)
    gate_local = contract_rows(normed16, grad_gate)
    normed_terms = contract_cols(grad_value, value_weight) + contract_cols(grad_gate, gate_weight)
    row_sums = stacked(jnp.sum(normed_terms, axis=1), jnp.sum(normed_terms * normed, axis=1))
    width_all = normed.shape[1]
    weight_parts = jnp.concatenate(
        [
            part.astype(jnp.bfloat16).reshape(shards, width_all // shards, part_width)
            for part in (value_local, gate_local, down_local)
        ],
        axis=1,
    )
    normed_parts, row_parts, weight_blocks = transfer(
        5,
        ("split", "tp", normed_terms.astype(jnp.bfloat16)),
        ("whole", "tp", row_sums),
        ("rows", "seq", weight_parts),
    )
    row_means = (summed(row_parts) / width_all).T
    normed_own = lax.dynamic_slice_in_dim(normed, tp_index * part_width, part_width, 1)
    grad_hidden = (summed(normed_parts) - row_means[:, 0:1] - normed_own * row_means[:, 1:2]) / sigma
    grad_packed = ((grad_out.astype(jnp.float32) + grad_hidden) * mask).astype(jnp.bfloat16)
    returned, mixed_parts = transfer(
        6,
        ("rows", "seq", grad_packed.reshape(shards, MOST, part_width)),
        ("split", "tp", mixed_local),
    )
    block_out = ((hidden_part.astype(jnp.float32) + summed(mixed_parts)) * mask).astype(
        jnp.bfloat16
    )
    value_grad, gate_grad, down_grad = jnp.split(summed(weight_blocks), 3, axis=0)
    row_ids = jnp.arange(own_rows, dtype=jnp.int32)
    clip_ends = offsets + clip_lens
    clip_of_row = jnp.sum((clip_ends[None, :] <= row_ids[:, None]).astype(jnp.int32), axis=1)
    row_match = clip_of_row[:, None] == shard_ids[None, :]
    row_start = jnp.sum(jnp.where(row_match, offsets[None, :], 0), axis=1)
    row_target = jnp.sum(jnp.where(row_match, clip_targets[None, :], 0), axis=1)
    positions = row_target * MOST + row_ids - row_start
    grad_proj = jnp.take(returned.reshape(shards * MOST, part_width), positions, axis=0)
    proj_local = contract_rows(subsampled, grad_proj)
    (proj_parts,) = transfer(
        7,
        (
            "rows",
            "seq",
            proj_local.astype(jnp.bfloat16).reshape(
                shards, proj_local.shape[0] // shards, part_width
            ),
        ),
    )
    proj_grad = summed(proj_parts)
    return (block_out, proj_grad, value_grad, gate_grad, down_grad, bn_gain_grad, bn_shift_grad)


def solution(mesh):
    placed = (
        P("seq", None),
        P(None, "tp"),
        P(None, "tp"),
        P(None, "tp"),
        P(None, "tp"),
        P("tp"),
        P("tp"),
        P(None, "tp"),
        P(),
        P(),
        P("seq", "tp"),
    )
    return jax.shard_map(
        body,
        mesh=mesh,
        in_specs=placed,
        out_specs=(
            P("seq", "tp"),
            P("seq", "tp"),
            P("seq", "tp"),
            P("seq", "tp"),
            P("seq", "tp"),
            P("tp"),
            P("tp"),
        ),
        check_vma=False,
    )
```

```python
import functools
import jax
import jax.numpy as jnp
from jax import lax
from jax.experimental import pallas as pl
from jax.experimental.pallas import tpu as pltpu
from jax.sharding import PartitionSpec as P

MOST = 64


PIECES = 4
GATHERS = ("columns", "whole", "deal")


def source_of(kind, ref, index):
    if kind == "rows":
        return ref.at[index]
    if kind == "split":
        width = ref.shape[1] // lax.axis_size("tp")
        return ref.at[:, pl.ds(pl.multiple_of(index * width, 128), width)]
    height = ref.shape[0] // lax.axis_size("tp")
    width = ref.shape[1] // lax.axis_size("seq")
    begin = pl.multiple_of(lax.axis_index("tp") * height, 16)
    return ref.at[pl.ds(begin, height), pl.ds(pl.multiple_of(index * width, 128), width)]


def pieces_of(kind, ref):
    return 1 if kind == "whole" and ref.shape[0] < 64 else PIECES


def piece_from(source, piece, pieces):
    height = source.shape[0] // pieces
    return source.at[pl.ds(piece * height, height)]


def piece_in(kind, target, source, index, piece, pieces):
    height = source.shape[0] // pieces
    rows = pl.ds(piece * height, height)
    if kind == "columns":
        width = source.shape[1]
        return target.at[rows, pl.ds(pl.multiple_of(index * width, 128), width)]
    if kind == "deal":
        return target.at[rows, index]
    return target.at[index, rows]


def push(source, target, send_sem, recv_sem, axis, peer):
    copy = pltpu.make_async_remote_copy(
        src_ref=source,
        dst_ref=target,
        send_sem=send_sem,
        recv_sem=recv_sem,
        device_id={axis: peer},
        device_id_type=pl.DeviceIdType.MESH,
    )
    copy.start()
    return copy


def transfer_kernel(plan, *refs):
    count = len(plan)
    sources, targets = refs[:count], refs[count : 2 * count]
    sends, recvs = refs[2 * count : 3 * count], refs[3 * count : 4 * count]
    local_sem = refs[4 * count]
    barrier = pltpu.get_barrier_semaphore()
    greeted = 0
    for axis in sorted({axis for _, axis in plan}):
        size = lax.axis_size(axis)
        me = lax.axis_index(axis)
        for step in range(1, size):
            peer = lax.rem(me + step, size)
            pl.semaphore_signal(
                barrier, inc=1, device_id={axis: peer}, device_id_type=pl.DeviceIdType.MESH
            )
        greeted += size - 1
    pl.semaphore_wait(barrier, greeted)
    copies = []
    relays = []
    for which, (kind, axis) in enumerate(plan):
        size = lax.axis_size(axis)
        me = lax.axis_index(axis)
        source, target = sources[which], targets[which]
        if kind in GATHERS:
            pieces = pieces_of(kind, source)
            partner = me + 1 - 2 * lax.rem(me, 2)
            for piece in range(pieces):
                block = piece_from(source, piece, pieces)
                place = piece_in(kind, target, source, me, piece, pieces)
                for hop in range(1, size // 2):
                    slot = hop * pieces + piece
                    peer = lax.rem(me + 2 * hop, size)
                    first = push(
                        block, place, sends[which].at[slot], recvs[which].at[slot], axis, peer
                    )
                    relays.append((first, which, hop, piece))
                copies.append(
                    push(block, place, sends[which].at[piece], recvs[which].at[piece], axis, partner)
                )
            if kind == "columns":
                width = source.shape[1]
                home = target.at[:, pl.ds(pl.multiple_of(me * width, 128), width)]
            elif kind == "deal":
                home = target.at[:, me]
            else:
                home = target.at[me]
            own = pltpu.make_async_copy(source, home, local_sem.at[which])
        else:
            for step in range(1, size):
                peer = lax.rem(me + step, size)
                copies.append(
                    push(
                        source_of(kind, source, peer),
                        target.at[me],
                        sends[which].at[step],
                        recvs[which].at[step],
                        axis,
                        peer,
                    )
                )
            own = pltpu.make_async_copy(
                source_of(kind, source, me), target.at[me], local_sem.at[which]
            )
        own.start()
        copies.append(own)
    for first, which, hop, piece in sorted(relays, key=lambda relay: relay[3]):
        kind, axis = plan[which]
        size = lax.axis_size(axis)
        me = lax.axis_index(axis)
        pieces = pieces_of(kind, sources[which])
        origin = lax.rem(me + size - 2 * hop, size)
        partner = me + 1 - 2 * lax.rem(me, 2)
        slot = (size // 2 + hop - 1) * pieces + piece
        first.wait_recv()
        place = piece_in(kind, targets[which], sources[which], origin, piece, pieces)
        copies.append(
            push(place, place, sends[which].at[slot], recvs[which].at[slot], axis, partner)
        )
    for first, _, _, _ in relays:
        first.wait_send()
    for copy in copies:
        copy.wait()


def transfer(number, *items):
    plan = tuple((kind, axis) for kind, axis, _ in items)
    arrays = [array for _, _, array in items]
    outs = []
    sems = []
    for kind, axis, array in items:
        size = lax.axis_size(axis)
        shape = array.shape
        if kind == "split":
            shape = (size, shape[0], shape[1] // size)
        elif kind == "columns":
            shape = (shape[0], shape[1] * size)
        elif kind == "quarter":
            shape = (size, shape[0] // lax.axis_size("tp"), shape[1] // size)
        elif kind == "deal":
            shape = (shape[0], size) + shape[1:]
        elif kind == "whole":
            shape = (size,) + shape
        outs.append(jax.ShapeDtypeStruct(shape, array.dtype))
        slots = size * pieces_of(kind, array) if kind in GATHERS else size
        sems.append(pltpu.SemaphoreType.DMA((slots,)))
    return pl.pallas_call(
        functools.partial(transfer_kernel, plan),
        out_shape=outs,
        in_specs=[pl.BlockSpec(memory_space=pl.ANY)] * len(arrays),
        out_specs=[pl.BlockSpec(memory_space=pl.ANY)] * len(arrays),
        scratch_shapes=sems + sems + [pltpu.SemaphoreType.DMA((len(plan),))],
        compiler_params=pltpu.CompilerParams(collective_id=number, has_side_effects=True),
    )(*arrays)


def summed(parts):
    return jnp.sum(parts.astype(jnp.float32), axis=0)


def stacked(first, second):
    empty = jnp.zeros((6,) + first.shape, jnp.float32)
    return jnp.concatenate([first[None], second[None], empty], axis=0)


def depthwise(field, kernel):
    half = kernel.shape[0] // 2
    length = field.shape[1]
    padded = jnp.pad(field, ((0, 0), (half, half), (0, 0)))
    total = jnp.zeros(field.shape, jnp.float32)
    for offset in range(kernel.shape[0]):
        total = total + kernel[offset] * padded[:, offset : offset + length]
    return total


def depthwise_back(grad, kernel):
    half = kernel.shape[0] // 2
    length = grad.shape[1]
    padded = jnp.pad(grad, ((0, 0), (half, half), (0, 0)))
    total = jnp.zeros(grad.shape, jnp.float32)
    for offset in range(kernel.shape[0]):
        begin = 2 * half - offset
        total = total + kernel[offset] * padded[:, begin : begin + length]
    return total


def contract_rows(left, right):
    return lax.dot_general(
        left, right, (((0,), (0,)), ((), ())), preferred_element_type=jnp.float32
    )


def contract_cols(left, right):
    return lax.dot_general(
        left, right, (((1,), (1,)), ((), ())), preferred_element_type=jnp.float32
    )


def body(
    subsampled,
    proj_weight,
    value_weight,
    gate_weight,
    conv_kernel,
    bn_gain,
    bn_shift,
    down_weight,
    clip_frames,
    clip_dest,
    out_grad,
):
    shards = lax.axis_size("seq")
    seq_index = lax.axis_index("seq")
    tp_index = lax.axis_index("tp")
    own_rows = subsampled.shape[0]
    part_width = proj_weight.shape[1]
    count = float(own_rows * shards)
    shard_ids = jnp.arange(shards, dtype=jnp.int32)
    earlier = shard_ids[None, :] < shard_ids[:, None]
    offsets = jnp.sum(jnp.where(earlier[None], clip_frames[:, None, :], 0), axis=2)
    row_ids = jnp.arange(own_rows, dtype=jnp.int32)[None, :, None]
    begins = offsets[:, None, :]
    inside = (row_ids >= begins) & (row_ids < begins + clip_frames[:, None, :])
    slot_of_row = jnp.sum(
        jnp.where(inside, clip_dest[:, None, :] * MOST + row_ids - begins, 0), axis=2
    )
    slot_ids = jnp.arange(shards * MOST, dtype=jnp.int32)
    frame_pos = jnp.arange(MOST, dtype=jnp.int32)
    own_slots = lax.dynamic_slice_in_dim(slot_of_row, seq_index, 1, 0)
    to_slots = (slot_ids[:, None] == own_slots).astype(jnp.bfloat16)
    projected = jnp.dot(subsampled, proj_weight, preferred_element_type=jnp.float32).astype(
        jnp.bfloat16
    )
    outgoing = jnp.dot(to_slots, projected, preferred_element_type=jnp.float32).astype(
        jnp.bfloat16
    )
    incoming = clip_dest == seq_index
    in_lengths = jnp.sum(jnp.where(incoming, clip_frames, 0), axis=1)
    valid = (frame_pos[None, :] < in_lengths[:, None]).reshape(-1, 1)
    mask = valid.astype(jnp.float32)
    grad_out = jnp.where(valid, out_grad, jnp.zeros((), jnp.bfloat16))
    arrived, grad_full = transfer(
        1,
        ("rows", "seq", outgoing.reshape(shards, MOST, part_width)),
        ("columns", "tp", grad_out),
    )
    hidden_part = arrived.reshape(shards * MOST, part_width)
    hidden_full, quarter = transfer(
        2, ("columns", "tp", hidden_part), ("quarter", "seq", subsampled)
    )
    hidden32 = hidden_full.astype(jnp.float32)
    centred = hidden32 - jnp.mean(hidden32, axis=1, keepdims=True)
    sigma = jnp.sqrt(jnp.mean(centred * centred, axis=1, keepdims=True) + 1e-05)
    normed = centred / sigma
    normed16 = normed.astype(jnp.bfloat16)
    value_pre = jnp.dot(normed16, value_weight, preferred_element_type=jnp.float32)
    gate_pre = jnp.dot(normed16, gate_weight, preferred_element_type=jnp.float32)
    gate_sig = jax.nn.sigmoid(gate_pre)
    glu = value_pre * gate_sig * mask
    conv = depthwise(glu.reshape(shards, MOST, part_width), conv_kernel).reshape(-1, part_width)
    (conv_parts,) = transfer(
        3, ("whole", "seq", stacked(jnp.sum(conv * mask, axis=0), jnp.sum(conv * conv * mask, axis=0)))
    )
    conv_sums = summed(conv_parts)
    conv_total, square_total = conv_sums[0], conv_sums[1]
    conv_mean = conv_total / count
    conv_var = square_total / count - conv_mean * conv_mean
    bn_scale = jnp.sqrt(conv_var + 1e-05)
    bn_hat = (conv - conv_mean) / bn_scale
    batch_normed = bn_gain * bn_hat + bn_shift
    bn_sig = jax.nn.sigmoid(batch_normed)
    swish = (batch_normed * bn_sig).astype(jnp.bfloat16)
    mixed_local = contract_cols(swish, down_weight).astype(jnp.bfloat16)
    down_local = contract_rows(grad_full, swish)
    grad_swish = jnp.dot(grad_full, down_weight, preferred_element_type=jnp.float32)
    grad_bn = grad_swish * bn_sig * (1.0 + batch_normed * (1.0 - bn_sig)) * mask
    (bn_parts,) = transfer(
        4, ("whole", "seq", stacked(jnp.sum(grad_bn, axis=0), jnp.sum(grad_bn * bn_hat, axis=0)))
    )
    bn_sums = summed(bn_parts)
    bn_shift_grad, bn_gain_grad = bn_sums[0], bn_sums[1]
    grad_conv = (
        bn_gain / bn_scale * (grad_bn - (bn_shift_grad + bn_hat * bn_gain_grad) / count) * mask
    )
    grad_glu = (
        depthwise_back(grad_conv.reshape(shards, MOST, part_width), conv_kernel).reshape(
            -1, part_width
        )
        * mask
    )
    grad_value = (grad_glu * gate_sig).astype(jnp.bfloat16)
    grad_gate = (grad_glu * value_pre * gate_sig * (1.0 - gate_sig)).astype(jnp.bfloat16)
    value_local = contract_rows(normed16, grad_value)
    gate_local = contract_rows(normed16, grad_gate)
    normed_terms = contract_cols(grad_value, value_weight) + contract_cols(grad_gate, gate_weight)
    row_sums = stacked(jnp.sum(normed_terms, axis=1), jnp.sum(normed_terms * normed, axis=1))
    width_all = normed.shape[1]
    weight_parts = jnp.concatenate(
        [
            part.astype(jnp.bfloat16).reshape(shards, width_all // shards, part_width)
            for part in (value_local, gate_local, down_local)
        ],
        axis=1,
    )
    normed_parts, row_parts, gathered_sub, weight_blocks = transfer(
        5,
        ("split", "tp", normed_terms.astype(jnp.bfloat16)),
        ("whole", "tp", row_sums),
        ("whole", "tp", quarter.reshape(-1, quarter.shape[2])),
        ("rows", "seq", weight_parts),
    )
    row_means = (summed(row_parts) / width_all).T
    normed_own = lax.dynamic_slice_in_dim(normed, tp_index * part_width, part_width, 1)
    grad_hidden = (summed(normed_parts) - row_means[:, 0:1] - normed_own * row_means[:, 1:2]) / sigma
    grad_packed = ((grad_out.astype(jnp.float32) + grad_hidden) * mask).astype(jnp.bfloat16)
    returned, mixed_parts = transfer(
        6,
        ("deal", "seq", grad_packed.reshape(shards, MOST, part_width)),
        ("split", "tp", mixed_local),
    )
    block_out = ((hidden_part.astype(jnp.float32) + summed(mixed_parts)) * mask).astype(
        jnp.bfloat16
    )
    value_grad, gate_grad, down_grad = jnp.split(summed(weight_blocks), 3, axis=0)
    returned = returned.reshape(shards, shards * MOST, part_width)
    if shards <= 8:
        to_rows = (slot_of_row[:, :, None] == slot_ids[None, None, :]).astype(jnp.bfloat16)
        grad_proj = lax.dot_general(
            to_rows,
            returned,
            (((2,), (1,)), ((0,), (0,))),
            preferred_element_type=jnp.float32,
        ).astype(jnp.bfloat16)
    else:
        grad_proj = jnp.take_along_axis(returned, slot_of_row[:, :, None], axis=1)
    ranks = lax.axis_size("tp")
    grad_proj = grad_proj.reshape(shards, ranks, own_rows // ranks, part_width)
    grad_proj = jnp.swapaxes(grad_proj, 0, 1).reshape(shards * own_rows, part_width)
    proj_grad = contract_rows(
        gathered_sub.reshape(shards * own_rows, gathered_sub.shape[2]), grad_proj
    )
    return (block_out, proj_grad, value_grad, gate_grad, down_grad, bn_gain_grad, bn_shift_grad)


def solution(mesh):
    placed = (
        P("seq", None),
        P(None, "tp"),
        P(None, "tp"),
        P(None, "tp"),
        P(None, "tp"),
        P("tp"),
        P("tp"),
        P(None, "tp"),
        P(),
        P(),
        P("seq", "tp"),
    )
    return jax.shard_map(
        body,
        mesh=mesh,
        in_specs=placed,
        out_specs=(
            P("seq", "tp"),
            P("seq", "tp"),
            P("seq", "tp"),
            P("seq", "tp"),
            P("seq", "tp"),
            P("tp"),
            P("tp"),
        ),
        check_vma=False,
    )
```

```python
import functools
import jax
import jax.numpy as jnp
from jax import lax
from jax.experimental import pallas as pl
from jax.experimental.pallas import tpu as pltpu
from jax.sharding import PartitionSpec as P

MOST = 64


PIECES = 4
GATHERS = ("columns", "whole", "deal")


def source_of(kind, ref, index):
    if kind == "rows":
        return ref.at[index]
    if kind == "small":
        return ref
    if kind == "split":
        width = ref.shape[1] // lax.axis_size("tp")
        return ref.at[:, pl.ds(pl.multiple_of(index * width, 128), width)]
    height = ref.shape[0] // lax.axis_size("tp")
    width = ref.shape[1] // lax.axis_size("seq")
    begin = pl.multiple_of(lax.axis_index("tp") * height, 16)
    return ref.at[pl.ds(begin, height), pl.ds(pl.multiple_of(index * width, 128), width)]


def pieces_of(kind, ref):
    return PIECES


def piece_from(source, piece, pieces):
    height = source.shape[0] // pieces
    return source.at[pl.ds(piece * height, height)]


def piece_in(kind, target, source, index, piece, pieces):
    height = source.shape[0] // pieces
    rows = pl.ds(piece * height, height)
    if kind == "columns":
        width = source.shape[1]
        return target.at[rows, pl.ds(pl.multiple_of(index * width, 128), width)]
    if kind == "deal":
        return target.at[rows, index]
    return target.at[index, rows]


def push(source, target, send_sem, recv_sem, axis, peer):
    copy = pltpu.make_async_remote_copy(
        src_ref=source,
        dst_ref=target,
        send_sem=send_sem,
        recv_sem=recv_sem,
        device_id={axis: peer},
        device_id_type=pl.DeviceIdType.MESH,
    )
    copy.start()
    return copy


def greet(axes):
    barrier = pltpu.get_barrier_semaphore()
    greeted = 0
    for axis in axes:
        size = lax.axis_size(axis)
        me = lax.axis_index(axis)
        for step in range(1, size):
            peer = lax.rem(me + step, size)
            pl.semaphore_signal(
                barrier, inc=1, device_id={axis: peer}, device_id_type=pl.DeviceIdType.MESH
            )
        greeted += size - 1
    pl.semaphore_wait(barrier, greeted)


def partner_of(me):
    return me + 1 - 2 * lax.rem(me, 2)


def start_gather(kind, axis, source, target, send, recv, local):
    size = lax.axis_size(axis)
    me = lax.axis_index(axis)
    pieces = pieces_of(kind, source)
    copies, relays = [], []
    for piece in range(pieces):
        block = piece_from(source, piece, pieces)
        place = piece_in(kind, target, source, me, piece, pieces)
        for hop in range(1, size // 2):
            slot = hop * pieces + piece
            peer = lax.rem(me + 2 * hop, size)
            first = push(block, place, send.at[slot], recv.at[slot], axis, peer)
            relays.append((piece, first, hop, (kind, axis, source, target, send, recv)))
        copies.append(push(block, place, send.at[piece], recv.at[piece], axis, partner_of(me)))
    if kind == "columns":
        width = source.shape[1]
        home = target.at[:, pl.ds(pl.multiple_of(me * width, 128), width)]
    elif kind == "deal":
        home = target.at[:, me]
    else:
        home = target.at[me]
    own = pltpu.make_async_copy(source, home, local)
    own.start()
    copies.append(own)
    return copies, relays


def relay_all(relays):
    copies = []
    for piece, first, hop, (kind, axis, source, target, send, recv) in sorted(
        relays, key=lambda relay: relay[0]
    ):
        size = lax.axis_size(axis)
        me = lax.axis_index(axis)
        pieces = pieces_of(kind, source)
        origin = lax.rem(me + size - 2 * hop, size)
        slot = (size // 2 + hop - 1) * pieces + piece
        first.wait_recv()
        place = piece_in(kind, target, source, origin, piece, pieces)
        copies.append(push(place, place, send.at[slot], recv.at[slot], axis, partner_of(me)))
    for _, first, _, _ in relays:
        first.wait_send()
    return copies


def start_direct(kind, axis, source, target, send, recv, local):
    size = lax.axis_size(axis)
    me = lax.axis_index(axis)
    copies = []
    for step in range(1, size):
        peer = lax.rem(me + step, size)
        block = source_of(kind, source, peer)
        copies.append(push(block, target.at[me], send.at[step], recv.at[step], axis, peer))
    own = pltpu.make_async_copy(source_of(kind, source, me), target.at[me], local)
    own.start()
    copies.append(own)
    return copies


def start_reduce(axis, source, landing, send, recv):
    half = lax.axis_size(axis) // 2
    me = lax.axis_index(axis)
    partner = partner_of(me)
    copies = []
    for step in range(half):
        line = lax.rem(me // 2 + 1 + step, half)
        block = source.at[2 * line + lax.rem(partner, 2)]
        copies.append(
            push(block, landing.at[step], send.at[step], recv.at[step], axis, partner)
        )
    return copies


def finish_reduce(axis, firsts, source, landing, partial, target, send, recv, local):
    half = lax.axis_size(axis) // 2
    me = lax.axis_index(axis)
    copies = []
    for step in range(half):
        line = lax.rem(me // 2 + 1 + step, half)
        peer = 2 * line + lax.rem(me, 2)
        firsts[step].wait()
        both = source[peer].astype(jnp.float32) + landing[step].astype(jnp.float32)
        partial[step] = both.astype(partial.dtype)
        place = target.at[me // 2]
        if step < half - 1:
            slot = half + step
            copies.append(
                push(partial.at[step], place, send.at[slot], recv.at[slot], axis, peer)
            )
        else:
            own = pltpu.make_async_copy(partial.at[step], place, local)
            own.start()
            copies.append(own)
    return copies


def transfer_kernel(plan, *refs):
    count = len(plan)
    sources, targets = refs[:count], refs[count : 2 * count]
    sends, recvs = refs[2 * count : 3 * count], refs[3 * count : 4 * count]
    local_sem = refs[4 * count]
    rooms = refs[4 * count + 1 :]
    greet(sorted({axis for _, axis in plan}))
    copies, relays, firsts, reduced = [], [], [], None
    for which, (kind, axis) in enumerate(plan):
        source, target = sources[which], targets[which]
        send, recv, local = sends[which], recvs[which], local_sem.at[which]
        if kind == "reduce":
            firsts = start_reduce(axis, source, rooms[0], send, recv)
            reduced = (axis, firsts, source, rooms[0], rooms[1], target, send, recv, local)
        elif kind in GATHERS:
            started, waiting = start_gather(kind, axis, source, target, send, recv, local)
            copies += started
            relays += waiting
        else:
            copies += start_direct(kind, axis, source, target, send, recv, local)
    if reduced is not None:
        copies += finish_reduce(*reduced)
    copies += relay_all(relays)
    for copy in copies:
        copy.wait()


def transfer(number, *items):
    plan = tuple((kind, axis) for kind, axis, _ in items)
    arrays = [array for _, _, array in items]
    outs, sems, specs, rooms = [], [], [], []
    for kind, axis, array in items:
        size = lax.axis_size(axis)
        shape = array.shape
        if kind == "split":
            shape = (size, shape[0], shape[1] // size)
        elif kind == "columns":
            shape = (shape[0], shape[1] * size)
        elif kind == "quarter":
            shape = (size, shape[0] // lax.axis_size("tp"), shape[1] // size)
        elif kind == "reduce":
            shape = (size // 2,) + shape[1:]
            rooms = [pltpu.VMEM(shape, array.dtype)] * 2
        elif kind in ("whole", "small"):
            shape = (size,) + shape
        outs.append(jax.ShapeDtypeStruct(shape, array.dtype))
        specs.append(pl.BlockSpec(memory_space=pltpu.VMEM if kind == "reduce" else pl.ANY))
        slots = size * pieces_of(kind, array) if kind in GATHERS else size
        sems.append(pltpu.SemaphoreType.DMA((slots,)))
    return pl.pallas_call(
        functools.partial(transfer_kernel, plan),
        out_shape=outs,
        in_specs=specs,
        out_specs=[pl.BlockSpec(memory_space=pl.ANY)] * len(arrays),
        scratch_shapes=sems + sems + [pltpu.SemaphoreType.DMA((len(plan),))] + rooms,
        compiler_params=pltpu.CompilerParams(collective_id=number, has_side_effects=True),
    )(*arrays)


def return_kernel(
    packed,
    to_rows,
    mixed,
    gathered,
    mixed_parts,
    landing,
    owned,
    packed_send,
    packed_recv,
    mixed_send,
    mixed_recv,
    owned_send,
    owned_recv,
    local_sem,
):
    greet(("seq", "tp"))
    arrivals = start_direct(
        "rows", "seq", packed, landing, packed_send, packed_recv, local_sem.at[0]
    )
    copies = start_direct("split", "tp", mixed, mixed_parts, mixed_send, mixed_recv, local_sem.at[1])
    for copy in arrivals:
        copy.wait()
    frames = landing[...].reshape(-1, landing.shape[2])
    rows = jnp.dot(to_rows[...], frames, preferred_element_type=jnp.float32)
    owned[...] = rows.astype(owned.dtype).reshape(owned.shape)
    started, relays = start_gather(
        "deal", "seq", owned, gathered, owned_send, owned_recv, local_sem.at[2]
    )
    copies += started
    copies += relay_all(relays)
    for copy in copies:
        copy.wait()


def send_back(number, packed, to_rows, mixed):
    shards = lax.axis_size("seq")
    ranks = lax.axis_size("tp")
    height = to_rows.shape[0] // ranks
    width = packed.shape[2]
    owned = (ranks, height, width)
    dma = pltpu.SemaphoreType.DMA
    return pl.pallas_call(
        return_kernel,
        out_shape=[
            jax.ShapeDtypeStruct((ranks, shards, height, width), packed.dtype),
            jax.ShapeDtypeStruct((ranks, mixed.shape[0], mixed.shape[1] // ranks), mixed.dtype),
        ],
        in_specs=[
            pl.BlockSpec(memory_space=pl.ANY),
            pl.BlockSpec(memory_space=pltpu.VMEM),
            pl.BlockSpec(memory_space=pl.ANY),
        ],
        out_specs=[pl.BlockSpec(memory_space=pl.ANY)] * 2,
        scratch_shapes=[
            pltpu.VMEM(packed.shape, packed.dtype),
            pltpu.VMEM(owned, packed.dtype),
            dma((shards,)),
            dma((shards,)),
            dma((ranks,)),
            dma((ranks,)),
            dma((shards * PIECES,)),
            dma((shards * PIECES,)),
            dma((3,)),
        ],
        compiler_params=pltpu.CompilerParams(collective_id=number, has_side_effects=True),
    )(packed, to_rows, mixed)


def summed(parts):
    return jnp.sum(parts.astype(jnp.float32), axis=0)


def stacked(first, second):
    empty = jnp.zeros((6,) + first.shape, jnp.float32)
    return jnp.concatenate([first[None], second[None], empty], axis=0)


def depthwise(field, kernel):
    half = kernel.shape[0] // 2
    length = field.shape[1]
    padded = jnp.pad(field, ((0, 0), (half, half), (0, 0)))
    total = jnp.zeros(field.shape, jnp.float32)
    for offset in range(kernel.shape[0]):
        total = total + kernel[offset] * padded[:, offset : offset + length]
    return total


def depthwise_back(grad, kernel):
    half = kernel.shape[0] // 2
    length = grad.shape[1]
    padded = jnp.pad(grad, ((0, 0), (half, half), (0, 0)))
    total = jnp.zeros(grad.shape, jnp.float32)
    for offset in range(kernel.shape[0]):
        begin = 2 * half - offset
        total = total + kernel[offset] * padded[:, begin : begin + length]
    return total


def contract_rows(left, right):
    return lax.dot_general(
        left, right, (((0,), (0,)), ((), ())), preferred_element_type=jnp.float32
    )


def contract_cols(left, right):
    return lax.dot_general(
        left, right, (((1,), (1,)), ((), ())), preferred_element_type=jnp.float32
    )


def body(
    subsampled,
    proj_weight,
    value_weight,
    gate_weight,
    conv_kernel,
    bn_gain,
    bn_shift,
    down_weight,
    clip_frames,
    clip_dest,
    out_grad,
):
    shards = lax.axis_size("seq")
    seq_index = lax.axis_index("seq")
    tp_index = lax.axis_index("tp")
    own_rows = subsampled.shape[0]
    part_width = proj_weight.shape[1]
    count = float(own_rows * shards)
    shard_ids = jnp.arange(shards, dtype=jnp.int32)
    earlier = shard_ids[None, :] < shard_ids[:, None]
    offsets = jnp.sum(jnp.where(earlier[None], clip_frames[:, None, :], 0), axis=2)
    row_ids = jnp.arange(own_rows, dtype=jnp.int32)[None, :, None]
    begins = offsets[:, None, :]
    inside = (row_ids >= begins) & (row_ids < begins + clip_frames[:, None, :])
    slot_of_row = jnp.sum(
        jnp.where(inside, clip_dest[:, None, :] * MOST + row_ids - begins, 0), axis=2
    )
    slot_ids = jnp.arange(shards * MOST, dtype=jnp.int32)
    frame_pos = jnp.arange(MOST, dtype=jnp.int32)
    own_slots = lax.dynamic_slice_in_dim(slot_of_row, seq_index, 1, 0)
    to_slots = (slot_ids[:, None] == own_slots).astype(jnp.bfloat16)
    projected = jnp.dot(subsampled, proj_weight, preferred_element_type=jnp.float32).astype(
        jnp.bfloat16
    )
    outgoing = jnp.dot(to_slots, projected, preferred_element_type=jnp.float32).astype(
        jnp.bfloat16
    )
    incoming = clip_dest == seq_index
    in_lengths = jnp.sum(jnp.where(incoming, clip_frames, 0), axis=1)
    valid = (frame_pos[None, :] < in_lengths[:, None]).reshape(-1, 1)
    mask = valid.astype(jnp.float32)
    grad_out = jnp.where(valid, out_grad, jnp.zeros((), jnp.bfloat16))
    arrived, grad_full = transfer(
        1,
        ("rows", "seq", outgoing.reshape(shards, MOST, part_width)),
        ("columns", "tp", grad_out),
    )
    hidden_part = arrived.reshape(shards * MOST, part_width)
    hidden_full, quarter = transfer(
        2, ("columns", "tp", hidden_part), ("quarter", "seq", subsampled)
    )
    hidden32 = hidden_full.astype(jnp.float32)
    centred = hidden32 - jnp.mean(hidden32, axis=1, keepdims=True)
    sigma = jnp.sqrt(jnp.mean(centred * centred, axis=1, keepdims=True) + 1e-05)
    normed = centred / sigma
    normed16 = normed.astype(jnp.bfloat16)
    value_pre = jnp.dot(normed16, value_weight, preferred_element_type=jnp.float32)
    gate_pre = jnp.dot(normed16, gate_weight, preferred_element_type=jnp.float32)
    gate_sig = jax.nn.sigmoid(gate_pre)
    glu = value_pre * gate_sig * mask
    conv = depthwise(glu.reshape(shards, MOST, part_width), conv_kernel).reshape(-1, part_width)
    (conv_parts,) = transfer(
        3, ("small", "seq", stacked(jnp.sum(conv * mask, axis=0), jnp.sum(conv * conv * mask, axis=0)))
    )
    conv_sums = summed(conv_parts)
    conv_total, square_total = conv_sums[0], conv_sums[1]
    conv_mean = conv_total / count
    conv_var = square_total / count - conv_mean * conv_mean
    bn_scale = jnp.sqrt(conv_var + 1e-05)
    bn_hat = (conv - conv_mean) / bn_scale
    batch_normed = bn_gain * bn_hat + bn_shift
    bn_sig = jax.nn.sigmoid(batch_normed)
    swish = (batch_normed * bn_sig).astype(jnp.bfloat16)
    mixed_local = contract_cols(swish, down_weight).astype(jnp.bfloat16)
    down_local = contract_rows(grad_full, swish)
    grad_swish = jnp.dot(grad_full, down_weight, preferred_element_type=jnp.float32)
    grad_bn = grad_swish * bn_sig * (1.0 + batch_normed * (1.0 - bn_sig)) * mask
    (bn_parts,) = transfer(
        4, ("small", "seq", stacked(jnp.sum(grad_bn, axis=0), jnp.sum(grad_bn * bn_hat, axis=0)))
    )
    bn_sums = summed(bn_parts)
    bn_shift_grad, bn_gain_grad = bn_sums[0], bn_sums[1]
    grad_conv = (
        bn_gain / bn_scale * (grad_bn - (bn_shift_grad + bn_hat * bn_gain_grad) / count) * mask
    )
    grad_glu = (
        depthwise_back(grad_conv.reshape(shards, MOST, part_width), conv_kernel).reshape(
            -1, part_width
        )
        * mask
    )
    grad_value = (grad_glu * gate_sig).astype(jnp.bfloat16)
    grad_gate = (grad_glu * value_pre * gate_sig * (1.0 - gate_sig)).astype(jnp.bfloat16)
    value_local = contract_rows(normed16, grad_value)
    gate_local = contract_rows(normed16, grad_gate)
    normed_terms = contract_cols(grad_value, value_weight) + contract_cols(grad_gate, gate_weight)
    row_sums = stacked(jnp.sum(normed_terms, axis=1), jnp.sum(normed_terms * normed, axis=1))
    width_all = normed.shape[1]
    weight_parts = jnp.concatenate(
        [
            part.astype(jnp.bfloat16).reshape(shards, width_all // shards, part_width)
            for part in (value_local, gate_local, down_local)
        ],
        axis=1,
    )
    normed_parts, row_parts, gathered_sub, weight_blocks = transfer(
        5,
        ("split", "tp", normed_terms.astype(jnp.bfloat16)),
        ("small", "tp", row_sums),
        ("whole", "tp", quarter.reshape(-1, quarter.shape[2])),
        ("reduce", "seq", weight_parts),
    )
    row_means = (summed(row_parts) / width_all).T
    normed_own = lax.dynamic_slice_in_dim(normed, tp_index * part_width, part_width, 1)
    grad_hidden = (summed(normed_parts) - row_means[:, 0:1] - normed_own * row_means[:, 1:2]) / sigma
    grad_packed = ((grad_out.astype(jnp.float32) + grad_hidden) * mask).astype(jnp.bfloat16)
    to_rows = (own_slots[0][:, None] == slot_ids[None, :]).astype(jnp.bfloat16)
    grad_proj, mixed_parts = send_back(
        6, grad_packed.reshape(shards, MOST, part_width), to_rows, mixed_local
    )
    block_out = ((hidden_part.astype(jnp.float32) + summed(mixed_parts)) * mask).astype(
        jnp.bfloat16
    )
    value_grad, gate_grad, down_grad = jnp.split(summed(weight_blocks), 3, axis=0)
    grad_proj = grad_proj.reshape(shards * own_rows, part_width)
    proj_grad = contract_rows(
        gathered_sub.reshape(shards * own_rows, gathered_sub.shape[2]), grad_proj
    )
    return (block_out, proj_grad, value_grad, gate_grad, down_grad, bn_gain_grad, bn_shift_grad)


def solution(mesh):
    placed = (
        P("seq", None),
        P(None, "tp"),
        P(None, "tp"),
        P(None, "tp"),
        P(None, "tp"),
        P("tp"),
        P("tp"),
        P(None, "tp"),
        P(),
        P(),
        P("seq", "tp"),
    )
    return jax.shard_map(
        body,
        mesh=mesh,
        in_specs=placed,
        out_specs=(
            P("seq", "tp"),
            P("seq", "tp"),
            P("seq", "tp"),
            P("seq", "tp"),
            P("seq", "tp"),
            P("tp"),
            P("tp"),
        ),
        check_vma=False,
    )
```

```python
import functools
import jax
import jax.numpy as jnp
from jax import lax
from jax.experimental import pallas as pl
from jax.experimental.pallas import tpu as pltpu
from jax.sharding import PartitionSpec as P

MOST = 64


PIECES = 4
GATHERS = ("columns", "whole", "deal")


def source_of(kind, ref, index):
    if kind == "rows":
        return ref.at[index]
    if kind == "small":
        return ref
    if kind == "split":
        width = ref.shape[1] // lax.axis_size("tp")
        return ref.at[:, pl.ds(pl.multiple_of(index * width, 128), width)]
    height = ref.shape[0] // lax.axis_size("tp")
    width = ref.shape[1] // lax.axis_size("seq")
    begin = pl.multiple_of(lax.axis_index("tp") * height, 16)
    return ref.at[pl.ds(begin, height), pl.ds(pl.multiple_of(index * width, 128), width)]


def pieces_of(kind, ref):
    return PIECES


def piece_from(source, piece, pieces):
    height = source.shape[0] // pieces
    return source.at[pl.ds(piece * height, height)]


def piece_in(kind, target, source, index, piece, pieces):
    height = source.shape[0] // pieces
    rows = pl.ds(piece * height, height)
    if kind == "columns":
        width = source.shape[1]
        return target.at[rows, pl.ds(pl.multiple_of(index * width, 128), width)]
    if kind == "deal":
        return target.at[rows, index]
    return target.at[index, rows]


def push(source, target, send_sem, recv_sem, axis, peer):
    copy = pltpu.make_async_remote_copy(
        src_ref=source,
        dst_ref=target,
        send_sem=send_sem,
        recv_sem=recv_sem,
        device_id={axis: peer},
        device_id_type=pl.DeviceIdType.MESH,
    )
    copy.start()
    return copy


def greet(axes):
    barrier = pltpu.get_barrier_semaphore()
    greeted = 0
    for axis in axes:
        size = lax.axis_size(axis)
        me = lax.axis_index(axis)
        for step in range(1, size):
            peer = lax.rem(me + step, size)
            pl.semaphore_signal(
                barrier, inc=1, device_id={axis: peer}, device_id_type=pl.DeviceIdType.MESH
            )
        greeted += size - 1
    pl.semaphore_wait(barrier, greeted)


def partner_of(me):
    return me + 1 - 2 * lax.rem(me, 2)


def start_gather(kind, axis, source, target, send, recv, local):
    size = lax.axis_size(axis)
    me = lax.axis_index(axis)
    pieces = pieces_of(kind, source)
    copies, relays = [], []
    for piece in range(pieces):
        block = piece_from(source, piece, pieces)
        place = piece_in(kind, target, source, me, piece, pieces)
        for hop in range(1, size // 2):
            slot = hop * pieces + piece
            peer = lax.rem(me + 2 * hop, size)
            first = push(block, place, send.at[slot], recv.at[slot], axis, peer)
            relays.append((piece, first, hop, (kind, axis, source, target, send, recv)))
        copies.append(push(block, place, send.at[piece], recv.at[piece], axis, partner_of(me)))
    if kind == "columns":
        width = source.shape[1]
        home = target.at[:, pl.ds(pl.multiple_of(me * width, 128), width)]
    elif kind == "deal":
        home = target.at[:, me]
    else:
        home = target.at[me]
    own = pltpu.make_async_copy(source, home, local)
    own.start()
    copies.append(own)
    return copies, relays


def relay_all(relays):
    copies = []
    for piece, first, hop, (kind, axis, source, target, send, recv) in sorted(
        relays, key=lambda relay: relay[0]
    ):
        size = lax.axis_size(axis)
        me = lax.axis_index(axis)
        pieces = pieces_of(kind, source)
        origin = lax.rem(me + size - 2 * hop, size)
        slot = (size // 2 + hop - 1) * pieces + piece
        first.wait_recv()
        place = piece_in(kind, target, source, origin, piece, pieces)
        copies.append(push(place, place, send.at[slot], recv.at[slot], axis, partner_of(me)))
    for _, first, _, _ in relays:
        first.wait_send()
    return copies


def start_direct(kind, axis, source, target, send, recv, local):
    size = lax.axis_size(axis)
    me = lax.axis_index(axis)
    copies = []
    for step in range(1, size):
        peer = lax.rem(me + step, size)
        block = source_of(kind, source, peer)
        copies.append(push(block, target.at[me], send.at[step], recv.at[step], axis, peer))
    own = pltpu.make_async_copy(source_of(kind, source, me), target.at[me], local)
    own.start()
    copies.append(own)
    return copies


def share_of(source, axis, index):
    if len(source.shape) == 3:
        return source.at[index]
    width = source.shape[1] // lax.axis_size(axis)
    return source.at[:, pl.ds(pl.multiple_of(index * width, 128), width)]


def start_reduce(axis, source, landing, send, recv):
    half = lax.axis_size(axis) // 2
    me = lax.axis_index(axis)
    partner = partner_of(me)
    copies = []
    for step in range(half):
        line = lax.rem(me // 2 + 1 + step, half)
        block = share_of(source, axis, 2 * line + lax.rem(partner, 2))
        copies.append(
            push(block, landing.at[step], send.at[step], recv.at[step], axis, partner)
        )
    return copies


def finish_reduce(axis, firsts, source, landing, partial, target, send, recv, local):
    half = lax.axis_size(axis) // 2
    me = lax.axis_index(axis)
    copies = []
    for step in range(half):
        line = lax.rem(me // 2 + 1 + step, half)
        peer = 2 * line + lax.rem(me, 2)
        firsts[step].wait()
        mine = share_of(source, axis, peer)[...]
        both = mine.astype(jnp.float32) + landing[step].astype(jnp.float32)
        partial[step] = both.astype(partial.dtype)
        place = target.at[me // 2]
        if step < half - 1:
            slot = half + step
            copies.append(
                push(partial.at[step], place, send.at[slot], recv.at[slot], axis, peer)
            )
        else:
            own = pltpu.make_async_copy(partial.at[step], place, local)
            own.start()
            copies.append(own)
    return copies


def transfer_kernel(plan, *refs):
    count = len(plan)
    sources, targets = refs[:count], refs[count : 2 * count]
    sends, recvs = refs[2 * count : 3 * count], refs[3 * count : 4 * count]
    local_sem = refs[4 * count]
    rooms = refs[4 * count + 1 :]
    greet(sorted({axis for _, axis in plan}))
    copies, relays, reduced = [], [], []
    for which, (kind, axis) in enumerate(plan):
        source, target = sources[which], targets[which]
        send, recv, local = sends[which], recvs[which], local_sem.at[which]
        if kind == "reduce":
            landing, partial = rooms[2 * len(reduced)], rooms[2 * len(reduced) + 1]
            firsts = start_reduce(axis, source, landing, send, recv)
            reduced.append((axis, firsts, source, landing, partial, target, send, recv, local))
        elif kind in GATHERS:
            started, waiting = start_gather(kind, axis, source, target, send, recv, local)
            copies += started
            relays += waiting
        else:
            copies += start_direct(kind, axis, source, target, send, recv, local)
    for state in reduced:
        copies += finish_reduce(*state)
    copies += relay_all(relays)
    for copy in copies:
        copy.wait()


def transfer(number, *items):
    plan = tuple((kind, axis) for kind, axis, _ in items)
    arrays = [array for _, _, array in items]
    outs, sems, specs, rooms = [], [], [], []
    for kind, axis, array in items:
        size = lax.axis_size(axis)
        shape = array.shape
        if kind == "split":
            shape = (size, shape[0], shape[1] // size)
        elif kind == "columns":
            shape = (shape[0], shape[1] * size)
        elif kind == "quarter":
            shape = (size, shape[0] // lax.axis_size("tp"), shape[1] // size)
        elif kind == "reduce":
            if len(shape) == 2:
                shape = (size // 2, shape[0], shape[1] // size)
            else:
                shape = (size // 2,) + shape[1:]
            rooms += [pltpu.VMEM(shape, array.dtype)] * 2
        elif kind in ("whole", "small"):
            shape = (size,) + shape
        outs.append(jax.ShapeDtypeStruct(shape, array.dtype))
        specs.append(pl.BlockSpec(memory_space=pltpu.VMEM if kind == "reduce" else pl.ANY))
        slots = size * pieces_of(kind, array) if kind in GATHERS else size
        sems.append(pltpu.SemaphoreType.DMA((slots,)))
    return pl.pallas_call(
        functools.partial(transfer_kernel, plan),
        out_shape=outs,
        in_specs=specs,
        out_specs=[pl.BlockSpec(memory_space=pl.ANY)] * len(arrays),
        scratch_shapes=sems + sems + [pltpu.SemaphoreType.DMA((len(plan),))] + rooms,
        compiler_params=pltpu.CompilerParams(collective_id=number, has_side_effects=True),
    )(*arrays)


def return_kernel(
    packed,
    to_rows,
    mixed,
    quarter,
    gathered,
    mixed_parts,
    sub,
    landing,
    owned,
    packed_send,
    packed_recv,
    mixed_send,
    mixed_recv,
    owned_send,
    owned_recv,
    sub_send,
    sub_recv,
    local_sem,
):
    greet(("seq", "tp"))
    arrivals = start_direct(
        "rows", "seq", packed, landing, packed_send, packed_recv, local_sem.at[0]
    )
    copies = start_direct("split", "tp", mixed, mixed_parts, mixed_send, mixed_recv, local_sem.at[1])
    sub_copies, sub_relays = start_gather(
        "whole", "tp", quarter, sub, sub_send, sub_recv, local_sem.at[3]
    )
    copies += sub_copies
    for copy in arrivals:
        copy.wait()
    frames = landing[...].reshape(-1, landing.shape[2])
    rows = jnp.dot(to_rows[...], frames, preferred_element_type=jnp.float32)
    owned[...] = rows.astype(owned.dtype).reshape(owned.shape)
    started, relays = start_gather(
        "deal", "seq", owned, gathered, owned_send, owned_recv, local_sem.at[2]
    )
    copies += started
    copies += relay_all(relays + sub_relays)
    for copy in copies:
        copy.wait()


def send_back(number, packed, to_rows, mixed, quarter):
    shards = lax.axis_size("seq")
    ranks = lax.axis_size("tp")
    height = to_rows.shape[0] // ranks
    width = packed.shape[2]
    owned = (ranks, height, width)
    dma = pltpu.SemaphoreType.DMA
    return pl.pallas_call(
        return_kernel,
        out_shape=[
            jax.ShapeDtypeStruct((ranks, shards, height, width), packed.dtype),
            jax.ShapeDtypeStruct((ranks, mixed.shape[0], mixed.shape[1] // ranks), mixed.dtype),
            jax.ShapeDtypeStruct((ranks,) + quarter.shape, quarter.dtype),
        ],
        in_specs=[
            pl.BlockSpec(memory_space=pl.ANY),
            pl.BlockSpec(memory_space=pltpu.VMEM),
            pl.BlockSpec(memory_space=pl.ANY),
            pl.BlockSpec(memory_space=pl.ANY),
        ],
        out_specs=[pl.BlockSpec(memory_space=pl.ANY)] * 3,
        scratch_shapes=[
            pltpu.VMEM(packed.shape, packed.dtype),
            pltpu.VMEM(owned, packed.dtype),
            dma((shards,)),
            dma((shards,)),
            dma((ranks,)),
            dma((ranks,)),
            dma((shards * PIECES,)),
            dma((shards * PIECES,)),
            dma((ranks * PIECES,)),
            dma((ranks * PIECES,)),
            dma((4,)),
        ],
        compiler_params=pltpu.CompilerParams(collective_id=number, has_side_effects=True),
    )(packed, to_rows, mixed, quarter)


def spread_kernel(
    outgoing,
    grad_out,
    subsampled,
    arrived,
    hidden,
    grad_full,
    quarter,
    out_send,
    out_recv,
    hidden_send,
    hidden_recv,
    grad_send,
    grad_recv,
    quarter_send,
    quarter_recv,
    block_sem,
    local_sem,
):
    greet(("seq", "tp"))
    shards, ranks = lax.axis_size("seq"), lax.axis_size("tp")
    me, rank = lax.axis_index("seq"), lax.axis_index("tp")
    height, width = outgoing.shape[1], outgoing.shape[2]
    arrivals = start_direct(
        "rows", "seq", outgoing, arrived, out_send, out_recv, local_sem.at[0]
    )
    copies, grad_relays = start_gather(
        "columns", "tp", grad_out, grad_full, grad_send, grad_recv, local_sem.at[1]
    )
    copies += start_direct(
        "quarter", "seq", subsampled, quarter, quarter_send, quarter_recv, local_sem.at[2]
    )

    def place_of(owner, column):
        rows = pl.ds(pl.multiple_of(owner * height, 16), height)
        return hidden.at[rows, pl.ds(pl.multiple_of(column * width, 128), width)]

    arrivals = arrivals[-1:] + arrivals[:-1]
    firsts = []
    for step in range(shards):
        owner = lax.rem(me + shards - step, shards)
        arrivals[step].wait()
        block, place = arrived.at[owner], place_of(owner, rank)
        for hop in range(1, ranks // 2):
            slot = hop * shards + step
            peer = lax.rem(rank + 2 * hop, ranks)
            first = push(block, place, hidden_send.at[slot], hidden_recv.at[slot], "tp", peer)
            firsts.append((first, owner, hop, step))
        copies.append(
            push(block, place, hidden_send.at[step], hidden_recv.at[step], "tp", partner_of(rank))
        )
        own = pltpu.make_async_copy(block, place, block_sem.at[step])
        own.start()
        copies.append(own)
    copies += relay_all(grad_relays)
    for first, owner, hop, step in firsts:
        first.wait()
        place = place_of(owner, lax.rem(rank + ranks - 2 * hop, ranks))
        slot = (ranks // 2 + hop - 1) * shards + step
        copies.append(
            push(
                place, place, hidden_send.at[slot], hidden_recv.at[slot], "tp", partner_of(rank)
            )
        )
    for copy in copies:
        copy.wait()


def spread(number, outgoing, grad_out, subsampled):
    shards, ranks = lax.axis_size("seq"), lax.axis_size("tp")
    full = (grad_out.shape[0], grad_out.shape[1] * ranks)
    quarter = (shards, subsampled.shape[0] // ranks, subsampled.shape[1] // shards)
    dma = pltpu.SemaphoreType.DMA
    return pl.pallas_call(
        spread_kernel,
        out_shape=[
            jax.ShapeDtypeStruct(outgoing.shape, outgoing.dtype),
            jax.ShapeDtypeStruct(full, outgoing.dtype),
            jax.ShapeDtypeStruct(full, grad_out.dtype),
            jax.ShapeDtypeStruct(quarter, subsampled.dtype),
        ],
        in_specs=[pl.BlockSpec(memory_space=pl.ANY)] * 3,
        out_specs=[pl.BlockSpec(memory_space=pl.ANY)] * 4,
        scratch_shapes=[
            dma((shards,)),
            dma((shards,)),
            dma((ranks * shards,)),
            dma((ranks * shards,)),
            dma((ranks * PIECES,)),
            dma((ranks * PIECES,)),
            dma((shards,)),
            dma((shards,)),
            dma((shards,)),
            dma((3,)),
        ],
        compiler_params=pltpu.CompilerParams(collective_id=number, has_side_effects=True),
    )(outgoing, grad_out, subsampled)


def summed(parts):
    return jnp.sum(parts.astype(jnp.float32), axis=0)


def stacked(first, second):
    empty = jnp.zeros((6,) + first.shape, jnp.float32)
    return jnp.concatenate([first[None], second[None], empty], axis=0)


def depthwise(field, kernel):
    half = kernel.shape[0] // 2
    length = field.shape[1]
    padded = jnp.pad(field, ((0, 0), (half, half), (0, 0)))
    total = jnp.zeros(field.shape, jnp.float32)
    for offset in range(kernel.shape[0]):
        total = total + kernel[offset] * padded[:, offset : offset + length]
    return total


def depthwise_back(grad, kernel):
    half = kernel.shape[0] // 2
    length = grad.shape[1]
    padded = jnp.pad(grad, ((0, 0), (half, half), (0, 0)))
    total = jnp.zeros(grad.shape, jnp.float32)
    for offset in range(kernel.shape[0]):
        begin = 2 * half - offset
        total = total + kernel[offset] * padded[:, begin : begin + length]
    return total


def contract_rows(left, right):
    return lax.dot_general(
        left, right, (((0,), (0,)), ((), ())), preferred_element_type=jnp.float32
    )


def contract_cols(left, right):
    return lax.dot_general(
        left, right, (((1,), (1,)), ((), ())), preferred_element_type=jnp.float32
    )


def body(
    subsampled,
    proj_weight,
    value_weight,
    gate_weight,
    conv_kernel,
    bn_gain,
    bn_shift,
    down_weight,
    clip_frames,
    clip_dest,
    out_grad,
):
    shards = lax.axis_size("seq")
    seq_index = lax.axis_index("seq")
    tp_index = lax.axis_index("tp")
    own_rows = subsampled.shape[0]
    part_width = proj_weight.shape[1]
    count = float(own_rows * shards)
    shard_ids = jnp.arange(shards, dtype=jnp.int32)
    earlier = shard_ids[None, :] < shard_ids[:, None]
    offsets = jnp.sum(jnp.where(earlier[None], clip_frames[:, None, :], 0), axis=2)
    row_ids = jnp.arange(own_rows, dtype=jnp.int32)[None, :, None]
    begins = offsets[:, None, :]
    inside = (row_ids >= begins) & (row_ids < begins + clip_frames[:, None, :])
    slot_of_row = jnp.sum(
        jnp.where(inside, clip_dest[:, None, :] * MOST + row_ids - begins, 0), axis=2
    )
    slot_ids = jnp.arange(shards * MOST, dtype=jnp.int32)
    frame_pos = jnp.arange(MOST, dtype=jnp.int32)
    own_slots = lax.dynamic_slice_in_dim(slot_of_row, seq_index, 1, 0)
    to_slots = (slot_ids[:, None] == own_slots).astype(jnp.bfloat16)
    projected = jnp.dot(subsampled, proj_weight, preferred_element_type=jnp.float32).astype(
        jnp.bfloat16
    )
    outgoing = jnp.dot(to_slots, projected, preferred_element_type=jnp.float32).astype(
        jnp.bfloat16
    )
    incoming = clip_dest == seq_index
    in_lengths = jnp.sum(jnp.where(incoming, clip_frames, 0), axis=1)
    valid = (frame_pos[None, :] < in_lengths[:, None]).reshape(-1, 1)
    mask = valid.astype(jnp.float32)
    grad_out = jnp.where(valid, out_grad, jnp.zeros((), jnp.bfloat16))
    arrived, hidden_full, grad_full, quarter = spread(
        1, outgoing.reshape(shards, MOST, part_width), grad_out, subsampled
    )
    hidden_part = arrived.reshape(shards * MOST, part_width)
    hidden32 = hidden_full.astype(jnp.float32)
    centred = hidden32 - jnp.mean(hidden32, axis=1, keepdims=True)
    sigma = jnp.sqrt(jnp.mean(centred * centred, axis=1, keepdims=True) + 1e-05)
    normed = centred / sigma
    normed16 = normed.astype(jnp.bfloat16)
    value_pre = jnp.dot(normed16, value_weight, preferred_element_type=jnp.float32)
    gate_pre = jnp.dot(normed16, gate_weight, preferred_element_type=jnp.float32)
    gate_sig = jax.nn.sigmoid(gate_pre)
    glu = value_pre * gate_sig * mask
    conv = depthwise(glu.reshape(shards, MOST, part_width), conv_kernel).reshape(-1, part_width)
    (conv_parts,) = transfer(
        3, ("small", "seq", stacked(jnp.sum(conv * mask, axis=0), jnp.sum(conv * conv * mask, axis=0)))
    )
    conv_sums = summed(conv_parts)
    conv_total, square_total = conv_sums[0], conv_sums[1]
    conv_mean = conv_total / count
    conv_var = square_total / count - conv_mean * conv_mean
    bn_scale = jnp.sqrt(conv_var + 1e-05)
    bn_hat = (conv - conv_mean) / bn_scale
    batch_normed = bn_gain * bn_hat + bn_shift
    bn_sig = jax.nn.sigmoid(batch_normed)
    swish = (batch_normed * bn_sig).astype(jnp.bfloat16)
    mixed_local = contract_cols(swish, down_weight).astype(jnp.bfloat16)
    down_local = contract_rows(grad_full, swish)
    grad_swish = jnp.dot(grad_full, down_weight, preferred_element_type=jnp.float32)
    grad_bn = grad_swish * bn_sig * (1.0 + batch_normed * (1.0 - bn_sig)) * mask
    (bn_parts,) = transfer(
        4, ("small", "seq", stacked(jnp.sum(grad_bn, axis=0), jnp.sum(grad_bn * bn_hat, axis=0)))
    )
    bn_sums = summed(bn_parts)
    bn_shift_grad, bn_gain_grad = bn_sums[0], bn_sums[1]
    grad_conv = (
        bn_gain / bn_scale * (grad_bn - (bn_shift_grad + bn_hat * bn_gain_grad) / count) * mask
    )
    grad_glu = (
        depthwise_back(grad_conv.reshape(shards, MOST, part_width), conv_kernel).reshape(
            -1, part_width
        )
        * mask
    )
    grad_value = (grad_glu * gate_sig).astype(jnp.bfloat16)
    grad_gate = (grad_glu * value_pre * gate_sig * (1.0 - gate_sig)).astype(jnp.bfloat16)
    value_local = contract_rows(normed16, grad_value)
    gate_local = contract_rows(normed16, grad_gate)
    normed_terms = contract_cols(grad_value, value_weight) + contract_cols(grad_gate, gate_weight)
    row_sums = stacked(jnp.sum(normed_terms, axis=1), jnp.sum(normed_terms * normed, axis=1))
    width_all = normed.shape[1]
    weight_parts = jnp.concatenate(
        [
            part.astype(jnp.bfloat16).reshape(shards, width_all // shards, part_width)
            for part in (value_local, gate_local, down_local)
        ],
        axis=1,
    )
    normed_parts, row_parts, weight_blocks = transfer(
        5,
        ("reduce", "tp", normed_terms.astype(jnp.bfloat16)),
        ("small", "tp", row_sums),
        ("reduce", "seq", weight_parts),
    )
    row_means = (summed(row_parts) / width_all).T
    normed_own = lax.dynamic_slice_in_dim(normed, tp_index * part_width, part_width, 1)
    grad_hidden = (summed(normed_parts) - row_means[:, 0:1] - normed_own * row_means[:, 1:2]) / sigma
    grad_packed = ((grad_out.astype(jnp.float32) + grad_hidden) * mask).astype(jnp.bfloat16)
    to_rows = (own_slots[0][:, None] == slot_ids[None, :]).astype(jnp.bfloat16)
    grad_proj, mixed_parts, gathered_sub = send_back(
        6,
        grad_packed.reshape(shards, MOST, part_width),
        to_rows,
        mixed_local,
        quarter.reshape(-1, quarter.shape[2]),
    )
    block_out = ((hidden_part.astype(jnp.float32) + summed(mixed_parts)) * mask).astype(
        jnp.bfloat16
    )
    value_grad, gate_grad, down_grad = jnp.split(summed(weight_blocks), 3, axis=0)
    grad_proj = grad_proj.reshape(shards * own_rows, part_width)
    proj_grad = contract_rows(
        gathered_sub.reshape(shards * own_rows, gathered_sub.shape[2]), grad_proj
    )
    return (block_out, proj_grad, value_grad, gate_grad, down_grad, bn_gain_grad, bn_shift_grad)


def solution(mesh):
    placed = (
        P("seq", None),
        P(None, "tp"),
        P(None, "tp"),
        P(None, "tp"),
        P(None, "tp"),
        P("tp"),
        P("tp"),
        P(None, "tp"),
        P(),
        P(),
        P("seq", "tp"),
    )
    return jax.shard_map(
        body,
        mesh=mesh,
        in_specs=placed,
        out_specs=(
            P("seq", "tp"),
            P("seq", "tp"),
            P("seq", "tp"),
            P("seq", "tp"),
            P("seq", "tp"),
            P("tp"),
            P("tp"),
        ),
        check_vma=False,
    )
```

```python
import functools
import jax
import jax.numpy as jnp
from jax import lax
from jax.experimental import pallas as pl
from jax.experimental.pallas import tpu as pltpu
from jax.sharding import PartitionSpec as P

MOST = 64


PIECES = 4
AHEAD = 2
GATHERS = ("columns", "whole", "deal")


def source_of(kind, ref, index):
    if kind == "rows":
        return ref.at[index]
    if kind == "small":
        return ref
    if kind == "split":
        width = ref.shape[1] // lax.axis_size("tp")
        return ref.at[:, pl.ds(pl.multiple_of(index * width, 128), width)]
    height = ref.shape[0] // lax.axis_size("tp")
    width = ref.shape[1] // lax.axis_size("seq")
    begin = pl.multiple_of(lax.axis_index("tp") * height, 16)
    return ref.at[pl.ds(begin, height), pl.ds(pl.multiple_of(index * width, 128), width)]


def pieces_of(kind, ref):
    return PIECES


def piece_from(source, piece, pieces):
    height = source.shape[0] // pieces
    return source.at[pl.ds(piece * height, height)]


def piece_in(kind, target, source, index, piece, pieces):
    height = source.shape[0] // pieces
    rows = pl.ds(piece * height, height)
    if kind == "columns":
        width = source.shape[1]
        return target.at[rows, pl.ds(pl.multiple_of(index * width, 128), width)]
    if kind == "deal":
        return target.at[rows, index]
    return target.at[index, rows]


def push(source, target, send_sem, recv_sem, axis, peer):
    copy = pltpu.make_async_remote_copy(
        src_ref=source,
        dst_ref=target,
        send_sem=send_sem,
        recv_sem=recv_sem,
        device_id={axis: peer},
        device_id_type=pl.DeviceIdType.MESH,
    )
    copy.start()
    return copy


def greet(axes):
    barrier = pltpu.get_barrier_semaphore()
    greeted = 0
    for axis in axes:
        size = lax.axis_size(axis)
        me = lax.axis_index(axis)
        for step in range(1, size):
            peer = lax.rem(me + step, size)
            pl.semaphore_signal(
                barrier, inc=1, device_id={axis: peer}, device_id_type=pl.DeviceIdType.MESH
            )
        greeted += size - 1
    pl.semaphore_wait(barrier, greeted)


def partner_of(me):
    return me + 1 - 2 * lax.rem(me, 2)


def start_gather(kind, axis, source, target, send, recv, local):
    size = lax.axis_size(axis)
    me = lax.axis_index(axis)
    pieces = pieces_of(kind, source)
    copies, relays = [], []
    for piece in range(pieces):
        block = piece_from(source, piece, pieces)
        place = piece_in(kind, target, source, me, piece, pieces)
        for hop in range(1, size // 2):
            slot = hop * pieces + piece
            peer = lax.rem(me + 2 * hop, size)
            start = functools.partial(
                push, block, place, send.at[slot], recv.at[slot], axis, peer
            )
            first = start() if piece < AHEAD else None
            relays.append([piece, first, hop, (kind, axis, source, target, send, recv), start])
        copies.append(push(block, place, send.at[piece], recv.at[piece], axis, partner_of(me)))
    if kind == "columns":
        width = source.shape[1]
        home = target.at[:, pl.ds(pl.multiple_of(me * width, 128), width)]
    elif kind == "deal":
        home = target.at[:, me]
    else:
        home = target.at[me]
    own = pltpu.make_async_copy(source, home, local)
    own.start()
    copies.append(own)
    return copies, relays


def relay_all(relays):
    copies = []
    for now in range(PIECES):
        for piece, first, hop, (kind, axis, source, target, send, recv), _ in relays:
            if piece != now:
                continue
            size = lax.axis_size(axis)
            me = lax.axis_index(axis)
            pieces = pieces_of(kind, source)
            origin = lax.rem(me + size - 2 * hop, size)
            slot = (size // 2 + hop - 1) * pieces + piece
            first.wait()
            place = piece_in(kind, target, source, origin, piece, pieces)
            copies.append(push(place, place, send.at[slot], recv.at[slot], axis, partner_of(me)))
        for relay in relays:
            if relay[0] == now + AHEAD:
                relay[1] = relay[4]()
    return copies


def start_direct(kind, axis, source, target, send, recv, local):
    size = lax.axis_size(axis)
    me = lax.axis_index(axis)
    copies = []
    for step in range(1, size):
        peer = lax.rem(me + step, size)
        block = source_of(kind, source, peer)
        copies.append(push(block, target.at[me], send.at[step], recv.at[step], axis, peer))
    own = pltpu.make_async_copy(source_of(kind, source, me), target.at[me], local)
    own.start()
    copies.append(own)
    return copies


def share_of(source, axis, index):
    if len(source.shape) == 3:
        return source.at[index]
    width = source.shape[1] // lax.axis_size(axis)
    return source.at[:, pl.ds(pl.multiple_of(index * width, 128), width)]


def pair_push(axis, source, landing, send, recv, step):
    half = lax.axis_size(axis) // 2
    me = lax.axis_index(axis)
    line = lax.rem(me // 2 + 1 + step, half)
    partner = partner_of(me)
    block = share_of(source, axis, 2 * line + lax.rem(partner, 2))
    return push(block, landing.at[step], send.at[step], recv.at[step], axis, partner)


def start_reduce(axis, source, landing, send, recv):
    first = min(AHEAD, lax.axis_size(axis) // 2)
    return [pair_push(axis, source, landing, send, recv, step) for step in range(first)]


def finish_reduce(axis, firsts, source, landing, partial, target, send, recv, local):
    half = lax.axis_size(axis) // 2
    me = lax.axis_index(axis)
    copies = []
    for step in range(half):
        line = lax.rem(me // 2 + 1 + step, half)
        peer = 2 * line + lax.rem(me, 2)
        firsts[step].wait()
        if step + AHEAD < half:
            firsts.append(pair_push(axis, source, landing, send, recv, step + AHEAD))
        mine = share_of(source, axis, peer)[...]
        both = mine.astype(jnp.float32) + landing[step].astype(jnp.float32)
        partial[step] = both.astype(partial.dtype)
        place = target.at[me // 2]
        if step < half - 1:
            slot = half + step
            copies.append(
                push(partial.at[step], place, send.at[slot], recv.at[slot], axis, peer)
            )
        else:
            own = pltpu.make_async_copy(partial.at[step], place, local)
            own.start()
            copies.append(own)
    return copies


def transfer_kernel(plan, *refs):
    count = len(plan)
    sources, targets = refs[:count], refs[count : 2 * count]
    sends, recvs = refs[2 * count : 3 * count], refs[3 * count : 4 * count]
    local_sem = refs[4 * count]
    rooms = refs[4 * count + 1 :]
    greet(sorted({axis for _, axis in plan}))
    copies, relays, reduced = [], [], []
    for which, (kind, axis) in enumerate(plan):
        source, target = sources[which], targets[which]
        send, recv, local = sends[which], recvs[which], local_sem.at[which]
        if kind == "reduce":
            landing, partial = rooms[2 * len(reduced)], rooms[2 * len(reduced) + 1]
            firsts = start_reduce(axis, source, landing, send, recv)
            reduced.append((axis, firsts, source, landing, partial, target, send, recv, local))
        elif kind in GATHERS:
            started, waiting = start_gather(kind, axis, source, target, send, recv, local)
            copies += started
            relays += waiting
        else:
            copies += start_direct(kind, axis, source, target, send, recv, local)
    for state in reduced:
        copies += finish_reduce(*state)
    copies += relay_all(relays)
    for copy in copies:
        copy.wait()


def transfer(number, *items):
    plan = tuple((kind, axis) for kind, axis, _ in items)
    arrays = [array for _, _, array in items]
    outs, sems, specs, rooms = [], [], [], []
    for kind, axis, array in items:
        size = lax.axis_size(axis)
        shape = array.shape
        if kind == "split":
            shape = (size, shape[0], shape[1] // size)
        elif kind == "columns":
            shape = (shape[0], shape[1] * size)
        elif kind == "quarter":
            shape = (size, shape[0] // lax.axis_size("tp"), shape[1] // size)
        elif kind == "reduce":
            if len(shape) == 2:
                shape = (size // 2, shape[0], shape[1] // size)
            else:
                shape = (size // 2,) + shape[1:]
            rooms += [pltpu.VMEM(shape, array.dtype)] * 2
        elif kind in ("whole", "small"):
            shape = (size,) + shape
        outs.append(jax.ShapeDtypeStruct(shape, array.dtype))
        specs.append(pl.BlockSpec(memory_space=pltpu.VMEM if kind == "reduce" else pl.ANY))
        slots = size * pieces_of(kind, array) if kind in GATHERS else size
        sems.append(pltpu.SemaphoreType.DMA((slots,)))
    return pl.pallas_call(
        functools.partial(transfer_kernel, plan),
        out_shape=outs,
        in_specs=specs,
        out_specs=[pl.BlockSpec(memory_space=pl.ANY)] * len(arrays),
        scratch_shapes=sems + sems + [pltpu.SemaphoreType.DMA((len(plan),))] + rooms,
        compiler_params=pltpu.CompilerParams(collective_id=number, has_side_effects=True),
    )(*arrays)


def return_kernel(
    packed,
    to_rows,
    quarter,
    gathered,
    sub,
    landing,
    owned,
    packed_send,
    packed_recv,
    owned_send,
    owned_recv,
    sub_send,
    sub_recv,
    local_sem,
):
    greet(("seq", "tp"))
    arrivals = start_direct(
        "rows", "seq", packed, landing, packed_send, packed_recv, local_sem.at[0]
    )
    copies, sub_relays = start_gather(
        "whole", "tp", quarter, sub, sub_send, sub_recv, local_sem.at[1]
    )
    for copy in arrivals:
        copy.wait()
    frames = landing[...].reshape(-1, landing.shape[2])
    rows = jnp.dot(to_rows[...], frames, preferred_element_type=jnp.float32)
    owned[...] = rows.astype(owned.dtype).reshape(owned.shape)
    started, relays = start_gather(
        "deal", "seq", owned, gathered, owned_send, owned_recv, local_sem.at[2]
    )
    copies += started
    copies += relay_all(relays + sub_relays)
    for copy in copies:
        copy.wait()


def send_back(number, packed, to_rows, quarter):
    shards = lax.axis_size("seq")
    ranks = lax.axis_size("tp")
    height = to_rows.shape[0] // ranks
    width = packed.shape[2]
    owned = (ranks, height, width)
    dma = pltpu.SemaphoreType.DMA
    return pl.pallas_call(
        return_kernel,
        out_shape=[
            jax.ShapeDtypeStruct((ranks, shards, height, width), packed.dtype),
            jax.ShapeDtypeStruct((ranks,) + quarter.shape, quarter.dtype),
        ],
        in_specs=[
            pl.BlockSpec(memory_space=pl.ANY),
            pl.BlockSpec(memory_space=pltpu.VMEM),
            pl.BlockSpec(memory_space=pl.ANY),
        ],
        out_specs=[pl.BlockSpec(memory_space=pl.ANY)] * 2,
        scratch_shapes=[
            pltpu.VMEM(packed.shape, packed.dtype),
            pltpu.VMEM(owned, packed.dtype),
            dma((shards,)),
            dma((shards,)),
            dma((shards * PIECES,)),
            dma((shards * PIECES,)),
            dma((ranks * PIECES,)),
            dma((ranks * PIECES,)),
            dma((3,)),
        ],
        compiler_params=pltpu.CompilerParams(collective_id=number, has_side_effects=True),
    )(packed, to_rows, quarter)


def spread_kernel(
    outgoing,
    grad_out,
    subsampled,
    arrived,
    hidden,
    grad_full,
    quarter,
    out_send,
    out_recv,
    hidden_send,
    hidden_recv,
    grad_send,
    grad_recv,
    quarter_send,
    quarter_recv,
    block_sem,
    local_sem,
):
    greet(("seq", "tp"))
    shards, ranks = lax.axis_size("seq"), lax.axis_size("tp")
    me, rank = lax.axis_index("seq"), lax.axis_index("tp")
    height, width = outgoing.shape[1], outgoing.shape[2]
    arrivals = start_direct(
        "rows", "seq", outgoing, arrived, out_send, out_recv, local_sem.at[0]
    )
    copies, grad_relays = start_gather(
        "columns", "tp", grad_out, grad_full, grad_send, grad_recv, local_sem.at[1]
    )

    def place_of(owner, column):
        rows = pl.ds(pl.multiple_of(owner * height, 16), height)
        return hidden.at[rows, pl.ds(pl.multiple_of(column * width, 128), width)]

    arrivals = arrivals[-1:] + arrivals[:-1]
    firsts = []
    for step in range(shards):
        owner = lax.rem(me + shards - step, shards)
        arrivals[step].wait()
        block, place = arrived.at[owner], place_of(owner, rank)
        for hop in range(1, ranks // 2):
            slot = hop * shards + step
            peer = lax.rem(rank + 2 * hop, ranks)
            first = push(block, place, hidden_send.at[slot], hidden_recv.at[slot], "tp", peer)
            firsts.append((first, owner, hop, step))
        copies.append(
            push(block, place, hidden_send.at[step], hidden_recv.at[step], "tp", partner_of(rank))
        )
        own = pltpu.make_async_copy(block, place, block_sem.at[step])
        own.start()
        copies.append(own)
    copies += start_direct(
        "quarter", "seq", subsampled, quarter, quarter_send, quarter_recv, local_sem.at[2]
    )
    copies += relay_all(grad_relays)
    for first, owner, hop, step in firsts:
        first.wait()
        place = place_of(owner, lax.rem(rank + ranks - 2 * hop, ranks))
        slot = (ranks // 2 + hop - 1) * shards + step
        copies.append(
            push(
                place, place, hidden_send.at[slot], hidden_recv.at[slot], "tp", partner_of(rank)
            )
        )
    for copy in copies:
        copy.wait()


def spread(number, outgoing, grad_out, subsampled):
    shards, ranks = lax.axis_size("seq"), lax.axis_size("tp")
    full = (grad_out.shape[0], grad_out.shape[1] * ranks)
    quarter = (shards, subsampled.shape[0] // ranks, subsampled.shape[1] // shards)
    dma = pltpu.SemaphoreType.DMA
    return pl.pallas_call(
        spread_kernel,
        out_shape=[
            jax.ShapeDtypeStruct(outgoing.shape, outgoing.dtype),
            jax.ShapeDtypeStruct(full, outgoing.dtype),
            jax.ShapeDtypeStruct(full, grad_out.dtype),
            jax.ShapeDtypeStruct(quarter, subsampled.dtype),
        ],
        in_specs=[pl.BlockSpec(memory_space=pl.ANY)] * 3,
        out_specs=[pl.BlockSpec(memory_space=pl.ANY)] * 4,
        scratch_shapes=[
            dma((shards,)),
            dma((shards,)),
            dma((ranks * shards,)),
            dma((ranks * shards,)),
            dma((ranks * PIECES,)),
            dma((ranks * PIECES,)),
            dma((shards,)),
            dma((shards,)),
            dma((shards,)),
            dma((3,)),
        ],
        compiler_params=pltpu.CompilerParams(collective_id=number, has_side_effects=True),
    )(outgoing, grad_out, subsampled)


def summed(parts):
    return jnp.sum(parts.astype(jnp.float32), axis=0)


def stacked(first, second):
    empty = jnp.zeros((6,) + first.shape, jnp.float32)
    return jnp.concatenate([first[None], second[None], empty], axis=0)


def depthwise(field, kernel):
    half = kernel.shape[0] // 2
    length = field.shape[1]
    padded = jnp.pad(field, ((0, 0), (half, half), (0, 0)))
    total = jnp.zeros(field.shape, jnp.float32)
    for offset in range(kernel.shape[0]):
        total = total + kernel[offset] * padded[:, offset : offset + length]
    return total


def depthwise_back(grad, kernel):
    half = kernel.shape[0] // 2
    length = grad.shape[1]
    padded = jnp.pad(grad, ((0, 0), (half, half), (0, 0)))
    total = jnp.zeros(grad.shape, jnp.float32)
    for offset in range(kernel.shape[0]):
        begin = 2 * half - offset
        total = total + kernel[offset] * padded[:, begin : begin + length]
    return total


def contract_rows(left, right):
    return lax.dot_general(
        left, right, (((0,), (0,)), ((), ())), preferred_element_type=jnp.float32
    )


def contract_cols(left, right):
    return lax.dot_general(
        left, right, (((1,), (1,)), ((), ())), preferred_element_type=jnp.float32
    )


def body(
    subsampled,
    proj_weight,
    value_weight,
    gate_weight,
    conv_kernel,
    bn_gain,
    bn_shift,
    down_weight,
    clip_frames,
    clip_dest,
    out_grad,
):
    shards = lax.axis_size("seq")
    seq_index = lax.axis_index("seq")
    tp_index = lax.axis_index("tp")
    own_rows = subsampled.shape[0]
    part_width = proj_weight.shape[1]
    count = float(own_rows * shards)
    shard_ids = jnp.arange(shards, dtype=jnp.int32)
    earlier = shard_ids[None, :] < shard_ids[:, None]
    offsets = jnp.sum(jnp.where(earlier[None], clip_frames[:, None, :], 0), axis=2)
    row_ids = jnp.arange(own_rows, dtype=jnp.int32)[None, :, None]
    begins = offsets[:, None, :]
    inside = (row_ids >= begins) & (row_ids < begins + clip_frames[:, None, :])
    slot_of_row = jnp.sum(
        jnp.where(inside, clip_dest[:, None, :] * MOST + row_ids - begins, 0), axis=2
    )
    slot_ids = jnp.arange(shards * MOST, dtype=jnp.int32)
    frame_pos = jnp.arange(MOST, dtype=jnp.int32)
    own_slots = lax.dynamic_slice_in_dim(slot_of_row, seq_index, 1, 0)
    to_slots = (slot_ids[:, None] == own_slots).astype(jnp.bfloat16)
    projected = jnp.dot(subsampled, proj_weight, preferred_element_type=jnp.float32).astype(
        jnp.bfloat16
    )
    outgoing = jnp.dot(to_slots, projected, preferred_element_type=jnp.float32).astype(
        jnp.bfloat16
    )
    incoming = clip_dest == seq_index
    in_lengths = jnp.sum(jnp.where(incoming, clip_frames, 0), axis=1)
    valid = (frame_pos[None, :] < in_lengths[:, None]).reshape(-1, 1)
    mask = valid.astype(jnp.float32)
    grad_out = jnp.where(valid, out_grad, jnp.zeros((), jnp.bfloat16))
    arrived, hidden_full, grad_full, quarter = spread(
        1, outgoing.reshape(shards, MOST, part_width), grad_out, subsampled
    )
    hidden_part = arrived.reshape(shards * MOST, part_width)
    hidden32 = hidden_full.astype(jnp.float32)
    centred = hidden32 - jnp.mean(hidden32, axis=1, keepdims=True)
    sigma = jnp.sqrt(jnp.mean(centred * centred, axis=1, keepdims=True) + 1e-05)
    normed = centred / sigma
    normed16 = normed.astype(jnp.bfloat16)
    value_pre = jnp.dot(normed16, value_weight, preferred_element_type=jnp.float32)
    gate_pre = jnp.dot(normed16, gate_weight, preferred_element_type=jnp.float32)
    gate_sig = jax.nn.sigmoid(gate_pre)
    glu = value_pre * gate_sig * mask
    conv = depthwise(glu.reshape(shards, MOST, part_width), conv_kernel).reshape(-1, part_width)
    (conv_parts,) = transfer(
        3, ("small", "seq", stacked(jnp.sum(conv * mask, axis=0), jnp.sum(conv * conv * mask, axis=0)))
    )
    conv_sums = summed(conv_parts)
    conv_total, square_total = conv_sums[0], conv_sums[1]
    conv_mean = conv_total / count
    conv_var = square_total / count - conv_mean * conv_mean
    bn_scale = jnp.sqrt(conv_var + 1e-05)
    bn_hat = (conv - conv_mean) / bn_scale
    batch_normed = bn_gain * bn_hat + bn_shift
    bn_sig = jax.nn.sigmoid(batch_normed)
    swish = (batch_normed * bn_sig).astype(jnp.bfloat16)
    mixed_local = contract_cols(swish, down_weight).astype(jnp.bfloat16)
    down_local = contract_rows(grad_full, swish)
    grad_swish = jnp.dot(grad_full, down_weight, preferred_element_type=jnp.float32)
    grad_bn = grad_swish * bn_sig * (1.0 + batch_normed * (1.0 - bn_sig)) * mask
    (bn_parts,) = transfer(
        4, ("small", "seq", stacked(jnp.sum(grad_bn, axis=0), jnp.sum(grad_bn * bn_hat, axis=0)))
    )
    bn_sums = summed(bn_parts)
    bn_shift_grad, bn_gain_grad = bn_sums[0], bn_sums[1]
    grad_conv = (
        bn_gain / bn_scale * (grad_bn - (bn_shift_grad + bn_hat * bn_gain_grad) / count) * mask
    )
    grad_glu = (
        depthwise_back(grad_conv.reshape(shards, MOST, part_width), conv_kernel).reshape(
            -1, part_width
        )
        * mask
    )
    grad_value = (grad_glu * gate_sig).astype(jnp.bfloat16)
    grad_gate = (grad_glu * value_pre * gate_sig * (1.0 - gate_sig)).astype(jnp.bfloat16)
    value_local = contract_rows(normed16, grad_value)
    gate_local = contract_rows(normed16, grad_gate)
    normed_terms = contract_cols(grad_value, value_weight) + contract_cols(grad_gate, gate_weight)
    row_sums = stacked(jnp.sum(normed_terms, axis=1), jnp.sum(normed_terms * normed, axis=1))
    width_all = normed.shape[1]
    weight_parts = jnp.concatenate(
        [
            part.astype(jnp.bfloat16).reshape(shards, width_all // shards, part_width)
            for part in (value_local, gate_local, down_local)
        ],
        axis=1,
    )
    normed_parts, row_parts, mixed_parts, weight_blocks = transfer(
        5,
        ("reduce", "tp", normed_terms.astype(jnp.bfloat16)),
        ("small", "tp", row_sums),
        ("reduce", "tp", mixed_local),
        ("reduce", "seq", weight_parts),
    )
    row_means = (summed(row_parts) / width_all).T
    normed_own = lax.dynamic_slice_in_dim(normed, tp_index * part_width, part_width, 1)
    grad_hidden = (summed(normed_parts) - row_means[:, 0:1] - normed_own * row_means[:, 1:2]) / sigma
    grad_packed = ((grad_out.astype(jnp.float32) + grad_hidden) * mask).astype(jnp.bfloat16)
    to_rows = (own_slots[0][:, None] == slot_ids[None, :]).astype(jnp.bfloat16)
    grad_proj, gathered_sub = send_back(
        6,
        grad_packed.reshape(shards, MOST, part_width),
        to_rows,
        quarter.reshape(-1, quarter.shape[2]),
    )
    block_out = ((hidden_part.astype(jnp.float32) + summed(mixed_parts)) * mask).astype(
        jnp.bfloat16
    )
    value_grad, gate_grad, down_grad = jnp.split(summed(weight_blocks), 3, axis=0)
    grad_proj = grad_proj.reshape(shards * own_rows, part_width)
    proj_grad = contract_rows(
        gathered_sub.reshape(shards * own_rows, gathered_sub.shape[2]), grad_proj
    )
    return (block_out, proj_grad, value_grad, gate_grad, down_grad, bn_gain_grad, bn_shift_grad)


def solution(mesh):
    placed = (
        P("seq", None),
        P(None, "tp"),
        P(None, "tp"),
        P(None, "tp"),
        P(None, "tp"),
        P("tp"),
        P("tp"),
        P(None, "tp"),
        P(),
        P(),
        P("seq", "tp"),
    )
    return jax.shard_map(
        body,
        mesh=mesh,
        in_specs=placed,
        out_specs=(
            P("seq", "tp"),
            P("seq", "tp"),
            P("seq", "tp"),
            P("seq", "tp"),
            P("seq", "tp"),
            P("tp"),
            P("tp"),
        ),
        check_vma=False,
    )
```
